32 devices in a mesh: groups: 2 (over x), ep: 16 (over z, y, core).
Axes of the slice: x: 2, y: 2, z: 4, core: 2. Of those that a mesh axis runs over, the one named last changes fastest.
Arguments:
- tokens: bfloat16 [2048, 7168], P(('groups', 'ep')), parts along dimension 0, may hold values from -6 to 6
- routes: int32 [2048, 4], P(('groups', 'ep')), parts along dimension 0, may hold values from 0 to 7, all different within a row; in each aligned block of 64 rows (0 to 63, 64 to 127, ...) at most 40 rows name the same one
- gates: float32 [2048, 4], P(('groups', 'ep')), parts along dimension 0, may hold values from 0.05 to 1
- w_gate: bfloat16 [16, 7168, 512], P('ep'), may hold values from -0.0625 to 0.0625
- w_up: bfloat16 [16, 7168, 512], P('ep'), may hold values from -0.0625 to 0.0625
- w_down: bfloat16 [16, 512, 7168], P('ep'), may hold values from -0.1875 to 0.1875
Outputs:
- mixed: bfloat16 [2048, 7168], P(('groups', 'ep')), parts along dimension 0
The draws below stay inside these ranges and needn't reach their ends.
There are 2 independent parts, one for each index of `groups`. The reference program is written for one: setup_inputs(seed, part) draws one part's arguments, and reference() takes and returns one part's arrays. A program takes and returns all parts, laid end to end along the dimension named above; an argument that names none is the same for every part. Nothing has to cross between parts.
Inputs may be any that keep to these rules, and one draw needn't show every extreme that they name: `routes`: each row names 4 different experts. Among the 64 rows of one device no expert is named more than 40 times, a bound that some block reaches.
All inputs are finite; a program needn't handle non-finite values.
Results may differ from the reference program's by a relative error of at most 0.0085.
The reference program's roundings to bfloat16 on the way count: a program that leaves them out, or rounds other values in their place, can miss the bound.
Values may be sent and summed in bfloat16 or wider, within the bound.
No kernel may reach another device: no remote copies, remote signals or barrier semaphores. Data moves between devices by JAX's collectives and lax.ppermute only.
A program may use at most 192 MiB of HBM per device.

```python
import math
import jax
import jax.numpy as jnp
import numpy as np
from jax import lax

D = 7168
HID = 1024
TOPK = 4
TOK_DEV = 64
EXPERTS = 8
SLICES = 16
HALF = 512
CAP = 40
TOKENS = 1024
N_EP = 16


def levels(stream_key, extent, cuts, least, top_value):
    def one(axis_at, blocks):
        steps = jax.random.uniform(jax.random.fold_in(jax.random.fold_in(stream_key, 6), axis_at), (blocks,), jnp.float32, least / len(cuts), top_value / len(cuts))
        return jnp.repeat(jnp.exp(steps), extent[axis_at] // blocks).reshape((-1,) + (1,) * (len(extent) - axis_at - 1))

    factor_of = one(*cuts[0])
    for cut in cuts[1:]:
        factor_of = factor_of * one(*cut)
    return factor_of


def shared_out(rng, own, number, rows, count, top, limit, lean):
    ranking = jax.random.permutation(rng, count)
    crowded, common = portions_of(count, rows * top, limit, lean, True), portions_of(count, rows * top, limit, lean, False)
    places = jnp.arange(count)

    def named(tallies, offset_by):
        used = int((tallies > 0).sum())
        fixed = max(1, used // 4)
        shifted = fixed + (places - fixed + offset_by * (used - fixed)) % max(1, count - fixed)
        return jnp.zeros((count,), jnp.int32).at[ranking[jnp.where(places < fixed, places, shifted)]].set(jnp.asarray(tallies, jnp.int32))

    tallies = jnp.where(number % 4 == 0, named(crowded, number // 4), named(common, number - number // 4 - 1))
    mixed = jax.random.permutation(jax.random.fold_in(own, 3), count)
    source_of, taker = mixed[0:count // 2 * 2:2], mixed[1:count // 2 * 2:2]
    margin = jnp.minimum(tallies[source_of] - 1, limit - tallies[taker]) // 2
    margin = jnp.where((source_of == ranking[0]) | (taker == ranking[0]) | (tallies[taker] == 0), 0, jnp.maximum(margin, 0))
    shifted = jax.random.randint(jax.random.fold_in(own, 4), (count // 2,), 0, 1 << 20) % (margin + 1)
    tallies = tallies.at[source_of].add(-shifted).at[taker].add(shifted)
    members = jnp.searchsorted(jnp.cumsum(tallies), jnp.arange(rows * top), side="right").astype(jnp.int32)
    table = members.reshape(top, rows).T
    table = table[jax.random.permutation(jax.random.fold_in(own, 1), rows)]
    offset_by = jax.random.randint(jax.random.fold_in(own, 2), (rows, 1), 0, top)
    return jnp.take_along_axis(table, (jnp.arange(top)[None, :] + offset_by) % top, axis=1)


def portions_of(count, total, most, lean, full):
    weights = [(1 << 20) // math.isqrt(standing ** lean) + 1 for standing in range(1, count + 1)]
    largest = most if full else min(most, max(-(-total // count), total * weights[0] // sum(weights)))
    least = 1 if total - largest >= count - 1 else 0
    holding, rest = [largest] + [least] * (count - 1), total - largest - least * (count - 1)
    while rest > 0:
        free = [i for i in range(1, count) if holding[i] < largest] or [i for i in range(1, count) if holding[i] < most]
        whole, left = sum([weights[i] for i in free]), rest
        for i in free:
            extra = min(most - holding[i], max(1, left * weights[i] // whole), rest)
            holding[i] = holding[i] + extra
            rest = rest - extra
    return np.array(holding)


def noise(stream_key, dims, width, limit, pieces=(), kind=jnp.bfloat16):
    result = width * jax.random.normal(stream_key, dims, jnp.float32)
    if pieces:
        result = result * levels(stream_key, dims, pieces, -0.22, 0.18)
    return jnp.clip(result, -limit, limit).astype(kind)


def setup_inputs(seed: int = 0, part: int = 0) -> dict:
    key_of = jax.random.split(jax.random.key(seed), 7)
    own_keys = jax.random.split(jax.random.fold_in(key_of[6], part), 7)
    tokens = noise(own_keys[0], (TOKENS, D), 1.0, 6.0, ((0, 16),))
    routes_keys = jax.random.split(jax.random.fold_in(own_keys[1], 1), TOKENS // TOK_DEV)
    routes_turns = jax.random.permutation(jax.random.fold_in(own_keys[1], 3), TOKENS // TOK_DEV)
    routes = jax.vmap(lambda own, number: shared_out(jax.random.fold_in(own_keys[1], 2), own, number, TOK_DEV, EXPERTS, TOPK, CAP, 2))(routes_keys, routes_turns).reshape((TOKENS, TOPK))
    gates = jnp.clip(jnp.exp(math.log(1.0) - 2.9957323 * jax.random.uniform(own_keys[2], (TOKENS, TOPK), jnp.float32) ** levels(own_keys[2], (TOKENS, TOPK), ((0, 16),), -0.2, 0.2)), 0.05, 1.0)
    w_gate = noise(key_of[3], (SLICES, D, HALF), D ** -0.5, 0.0625, ((0, 16),))
    w_up = noise(key_of[4], (SLICES, D, HALF), D ** -0.5, 0.0625, ((0, 16),))
    w_down = noise(key_of[5], (SLICES, HALF, D), HID ** -0.5, 0.1875, ((0, 16),))
    return dict(tokens=tokens, routes=routes, gates=gates, w_gate=w_gate, w_up=w_up, w_down=w_down)


def to_grid(values):
    magnitude = jnp.abs(values)
    spacing = jnp.full(values.shape, 2.0 ** -9, jnp.float32)
    for exponent in range(-5, 9):
        spacing = jnp.where(magnitude >= 2.0 ** exponent, spacing * 2.0, spacing)
    grid_value = jnp.floor(magnitude / spacing + 0.5) * spacing
    return jnp.where(values < 0, -grid_value, grid_value)


def quantize(rows):
    row_count = rows.shape[0]
    feature_count = rows.shape[1]
    blocks = rows.astype(jnp.float32).reshape(row_count, feature_count // 128, 128)
    largest = jnp.max(jnp.abs(blocks), axis=2)
    scales = ((largest + 1e-6) / 448.0).astype(jnp.bfloat16)
    scales = lax.optimization_barrier(scales)
    quantized = to_grid(blocks / scales.astype(jnp.float32)[:, :, None]).astype(jnp.bfloat16)
    return quantized.reshape(row_count, feature_count), scales


def restore(quantized, scales):
    row_count = quantized.shape[0]
    feature_count = quantized.shape[1]
    blocks = quantized.astype(jnp.float32).reshape(row_count, feature_count // 128, 128)
    restored = (blocks * scales.astype(jnp.float32)[:, :, None]).astype(jnp.bfloat16)
    return restored.reshape(row_count, feature_count)


def half_output(inputs, gate_slice, up_slice, down_slice):
    gate_part = jnp.dot(inputs, gate_slice, preferred_element_type=jnp.float32)
    up_part = jnp.dot(inputs, up_slice, preferred_element_type=jnp.float32)
    hidden = (jax.nn.silu(gate_part) * up_part).astype(jnp.bfloat16)
    partial_value = jnp.dot(hidden, down_slice, preferred_element_type=jnp.float32).astype(jnp.bfloat16)
    return lax.optimization_barrier(partial_value).astype(jnp.float32)


def reference(tokens, routes, gates, w_gate, w_up, w_down):
    quantized, scales = quantize(tokens)
    restored = restore(quantized, scales)
    row_bound = N_EP * CAP

    def one_expert(totals, operands):
        expert_id, gate_pair, up_pair, down_pair = operands
        chosen = routes == expert_id
        weighting = jnp.sum(jnp.where(chosen, gates, 0.0), axis=1)
        routed = jnp.any(chosen, axis=1)
        row_index = jnp.nonzero(routed, size=row_bound, fill_value=0)[0].astype(jnp.int32)
        present = jnp.arange(row_bound) < jnp.sum(routed.astype(jnp.int32))
        inputs = restored[row_index]
        first_half = half_output(inputs, gate_pair[0], up_pair[0], down_pair[0])
        second_half = half_output(inputs, gate_pair[1], up_pair[1], down_pair[1])
        combined = (first_half + second_half).astype(jnp.bfloat16)
        combined = lax.optimization_barrier(combined).astype(jnp.float32)
        factor = jnp.where(present, weighting[row_index], 0.0)
        return totals.at[row_index].add(factor[:, None] * combined), None

    initial = jnp.zeros((TOKENS, D), jnp.float32)
    operands = (jnp.arange(EXPERTS, dtype=jnp.int32),
                w_gate.reshape(EXPERTS, 2, D, HALF),
                w_up.reshape(EXPERTS, 2, D, HALF),
                w_down.reshape(EXPERTS, 2, HALF, D))
    totals, _ = lax.scan(one_expert, initial, operands)
    return totals.astype(jnp.bfloat16)
```

```python
import functools

import jax
import jax.numpy as jnp
from jax import lax
from jax.experimental import pallas as pl
from jax.experimental.pallas import tpu as pltpu
from jax.sharding import PartitionSpec as P

F32 = jnp.float32
BF16 = jnp.bfloat16
LANES = 128
BLOCK = 128
VMEM_LIMIT = 56 * 1024 * 1024


def whole_block(shape):
    return pl.BlockSpec(shape, lambda *_: (0,) * len(shape))


def params(grid_dims=0):
    if grid_dims:
        return pltpu.CompilerParams(
            vmem_limit_bytes=VMEM_LIMIT, dimension_semantics=("arbitrary",) * grid_dims
        )
    return pltpu.CompilerParams(vmem_limit_bytes=VMEM_LIMIT)


def to_grid(values):
    magnitude = jnp.abs(values)
    spacing = jnp.full(values.shape, 2.0 ** (-9), F32)
    inverse = jnp.full(values.shape, 2.0**9, F32)
    for exponent in range(-5, 9):
        above = magnitude >= 2.0**exponent
        spacing = jnp.where(above, 2.0 ** (exponent - 3), spacing)
        inverse = jnp.where(above, 2.0 ** (3 - exponent), inverse)
    grid_value = jnp.floor(magnitude * inverse + 0.5) * spacing
    return jnp.where(values < 0, -grid_value, grid_value)


def gate_of(ext, expert, experts):
    lane = lax.broadcasted_iota(jnp.int32, ext.shape, 1)
    mine = (lane == expert) | (lane == expert + experts) | (lane == expert + 2 * experts)
    return jnp.sum(jnp.where(mine, ext.astype(F32), 0.0), axis=1, keepdims=True)


def placement(gate, capacity):
    rows = gate.shape[0]
    routed = gate > 0.0
    before = lax.broadcasted_iota(jnp.int32, (rows, rows), 1) < lax.broadcasted_iota(
        jnp.int32, (rows, rows), 0
    )
    ones = jnp.broadcast_to(jnp.where(routed, 1.0, 0.0), (rows, LANES)).astype(BF16)
    rank = jnp.dot(jnp.where(before, 1.0, 0.0).astype(BF16), ones, preferred_element_type=F32)
    rank = rank[:, :1].astype(jnp.int32)
    place = lax.broadcasted_iota(jnp.int32, (rows, capacity), 1)
    return jnp.where(routed & (rank == place), 1.0, 0.0).astype(BF16)


def pick_rows(onehot, rows):
    return lax.dot_general(
        onehot, rows, (((0,), (0,)), ((), ())), preferred_element_type=F32
    ).astype(BF16)


def prepare_kernel(experts, capacity, at_ref, tokens_ref, routes_ref, gates_ref, x_ref, y_ref):
    rows, features = tokens_ref.shape
    lane = lax.broadcasted_iota(jnp.int32, (rows, LANES), 1)
    routes = routes_ref[...]
    gates = gates_ref[...]
    value = jnp.zeros((rows, LANES), F32)
    for k in range(routes.shape[1]):
        hit = (
            (lane == routes[:, k : k + 1])
            | (lane == routes[:, k : k + 1] + experts)
            | (lane == routes[:, k : k + 1] + 2 * experts)
        )
        value = value + jnp.where(hit, gates[:, k : k + 1], 0.0)
    high = value.astype(BF16).astype(F32)
    middle = (value - high).astype(BF16).astype(F32)
    low = value - high - middle
    ext = jnp.where(lane < experts, high, jnp.where(lane < 2 * experts, middle, low)).astype(BF16)
    onehot = placement(gate_of(ext, at_ref[1], experts), capacity)
    x_ref[:, features:] = ext
    y_ref[:, features:] = pick_rows(onehot, ext)
    step = 4 * BLOCK

    def body(i, carry):
        start = pl.multiple_of(i * step, step)
        parts = []
        for b in range(step // BLOCK):
            block = tokens_ref[:, pl.ds(pl.multiple_of(start + b * BLOCK, BLOCK), BLOCK)].astype(F32)
            largest = jnp.max(jnp.abs(block), axis=1, keepdims=True)
            scale = ((largest + 1e-06) / 448.0).astype(BF16).astype(F32)
            parts.append((to_grid(block / scale) * scale).astype(BF16))
        restored = jnp.concatenate(parts, axis=1)
        x_ref[:, pl.ds(start, step)] = restored
        y_ref[:, pl.ds(start, step)] = pick_rows(onehot, restored)
        return carry

    lax.fori_loop(0, features // step, body, 0)


def prepare(at, tokens, routes, gates, experts, capacity):
    rows, features = tokens.shape
    width = features + LANES
    return pl.pallas_call(
        functools.partial(prepare_kernel, experts, capacity),
        out_shape=(
            jax.ShapeDtypeStruct((rows, width), BF16),
            jax.ShapeDtypeStruct((capacity, width), BF16),
        ),
        in_specs=[pl.BlockSpec(memory_space=pltpu.SMEM)]
        + [pl.BlockSpec(memory_space=pltpu.VMEM)] * 3,
        out_specs=(pl.BlockSpec(memory_space=pltpu.VMEM),) * 2,
        compiler_params=params(),
        name="prepare",
    )(at, tokens, routes, gates)


def compact_kernel(experts, capacity, count, sums, at_ref, *refs):
    ins, outs = refs[:count], refs[count:]
    features = ins[0].shape[1] - LANES
    step = 1024
    pieces = []
    if sums:
        merged = outs[1]
        merged[...] = ins[0][...] + ins[1][...]
        sources = (merged,)
    else:
        sources = ins
    for j, source in enumerate(sources):
        onehot = placement(gate_of(source[:, features:], at_ref[1], experts), capacity)
        outs[0][j, :, features:] = pick_rows(onehot, source[:, features:])
        for start in range(0, features, step):
            outs[0][j, :, start : start + step] = pick_rows(onehot, source[:, start : start + step])


def compact(at, blocks, experts, capacity, sums=False):
    rows, width = blocks[0].shape
    count = len(blocks)
    out_shape = [jax.ShapeDtypeStruct((1 if sums else count, capacity, width), BF16)]
    if sums:
        out_shape.append(jax.ShapeDtypeStruct((rows, width), BF16))
    return pl.pallas_call(
        functools.partial(compact_kernel, experts, capacity, count, sums),
        out_shape=tuple(out_shape),
        in_specs=[pl.BlockSpec(memory_space=pltpu.SMEM)]
        + [pl.BlockSpec(memory_space=pltpu.VMEM)] * count,
        out_specs=(pl.BlockSpec(memory_space=pltpu.VMEM),) * len(out_shape),
        compiler_params=params(),
        name="compact",
    )(at, *blocks)


def expert_kernel(experts, full, extra, k_steps, at_ref, *refs):
    count = len(full) + len(extra)
    rows_in, refs = refs[:count], refs[count:]
    exts, refs = refs[:count], refs[count:]
    gate_own, gate_other, up_own, up_other, down_own, down_other = refs[:6]
    outs, (acc, hidden, weight) = refs[6 : 6 + count], refs[6 + count :]
    i = pl.program_id(0)
    half = gate_own.shape[2]
    pieces = []
    for j, size in enumerate(full):
        pieces.append((j, None, size))
    for j, (blocks, size) in enumerate(extra):
        for b in range(blocks):
            pieces.append((len(full) + j, b, size))

    def load(source, j, b):
        return source[j][...] if b is None else source[j][b]

    @pl.when(i == 0)
    def _():
        acc[...] = jnp.zeros_like(acc)
        weight[...] = jnp.concatenate(
            [
                jnp.broadcast_to(gate_of(load(exts, j, b), at_ref[0], experts), (size, LANES))
                for j, b, size in pieces
            ],
            axis=0,
        )

    @pl.when(i < k_steps)
    def _():
        x = jnp.concatenate([load(rows_in, j, b).astype(F32) for j, b, _ in pieces], axis=0)
        x = x.astype(BF16)
        for n, ref in enumerate((gate_own, gate_other, up_own, up_other)):
            acc[:, n * half : (n + 1) * half] += jnp.dot(x, ref[0], preferred_element_type=F32)

    @pl.when(i == k_steps - 1)
    def _():
        gate_part = acc[:, : 2 * half]
        hidden[...] = (jax.nn.silu(gate_part) * acc[:, 2 * half :]).astype(BF16)

    @pl.when(i >= k_steps)
    def _():
        own = jnp.dot(hidden[:, :half], down_own[0], preferred_element_type=F32)
        other = jnp.dot(hidden[:, half:], down_other[0], preferred_element_type=F32)
        total = own.astype(BF16).astype(F32) + other.astype(BF16).astype(F32)
        scaled = total.astype(BF16).astype(F32) * weight[:, :1]
        offset = 0
        for j, b, size in pieces:
            part = scaled[offset : offset + size].astype(BF16)
            if b is None:
                outs[j][...] = part
            else:
                outs[j][b] = part
            offset += size


def run_expert(at, full, extra, weights, experts, tile=1024):
    own, other = weights
    features, half = own[0].shape[1:]
    k_steps = features // tile
    n_steps = features // tile
    last = features // LANES
    inputs = list(full) + list(extra)
    row_specs, ext_specs, out_specs, out_shape = [], [], [], []
    for array in inputs:
        lead = array.shape[:-1]
        zeros = (0,) * len(lead)
        row_specs.append(
            pl.BlockSpec(lead + (tile,), lambda i, z=zeros: z + (jnp.minimum(i, k_steps - 1),))
        )
        ext_specs.append(pl.BlockSpec(lead + (LANES,), lambda i, z=zeros: z + (last,)))
        out_specs.append(
            pl.BlockSpec(lead + (tile,), lambda i, z=zeros: z + (jnp.maximum(i - k_steps, 0),))
        )
        out_shape.append(jax.ShapeDtypeStruct(lead + (features,), BF16))
    up_spec = pl.BlockSpec((1, tile, half), lambda i: (0, jnp.minimum(i, k_steps - 1), 0))
    down_spec = pl.BlockSpec((1, half, tile), lambda i: (0, 0, jnp.maximum(i - k_steps, 0)))
    total = sum(a.size // a.shape[-1] for a in inputs)
    return pl.pallas_call(
        functools.partial(
            expert_kernel,
            experts,
            tuple(a.shape[0] for a in full),
            tuple(a.shape[:2] for a in extra),
            k_steps,
        ),
        out_shape=tuple(out_shape),
        grid=(k_steps + n_steps,),
        in_specs=[pl.BlockSpec(memory_space=pltpu.SMEM)]
        + row_specs
        + ext_specs
        + [up_spec] * 4
        + [down_spec] * 2,
        out_specs=tuple(out_specs),
        scratch_shapes=[
            pltpu.VMEM((total, 4 * half), F32),
            pltpu.VMEM((total, 2 * half), BF16),
            pltpu.VMEM((total, LANES), F32),
        ],
        compiler_params=params(1),
        cost_estimate=pl.CostEstimate(
            flops=12 * total * features * half,
            bytes_accessed=12 * features * half + 4 * total * features,
            transcendentals=2 * total * half,
        ),
        name="expert",
    )(at, *inputs, *inputs, own[0], other[0], own[1], other[1], own[2], other[2])


def combine_kernel(experts, capacity, adds, at_ref, ext_ref, mine_ref, theirs_ref, *refs):
    out_ref, onehot = refs[adds], refs[adds + 1]

    @pl.when(pl.program_id(0) == 0)
    def _():
        gate = gate_of(ext_ref[...], at_ref[1], experts)
        onehot[...] = placement(gate, capacity).astype(F32)

    total = mine_ref[...].astype(F32) + jnp.dot(
        onehot[...].astype(BF16), theirs_ref[0], preferred_element_type=F32
    )
    for ref in refs[:adds]:
        total = total + ref[...].astype(F32)
    out_ref[...] = total.astype(BF16)


def combine(at, block, mine, theirs, index, adds, experts, tile=1792):
    rows, features = mine.shape
    capacity = theirs.shape[1]
    last = features // LANES
    spec = pl.BlockSpec((rows, tile), lambda i: (0, i))
    return pl.pallas_call(
        functools.partial(combine_kernel, experts, capacity, len(adds)),
        out_shape=jax.ShapeDtypeStruct((rows, features), BF16),
        grid=(features // tile,),
        in_specs=[
            pl.BlockSpec(memory_space=pltpu.SMEM),
            pl.BlockSpec((rows, LANES), lambda i: (0, last)),
            spec,
            pl.BlockSpec((1, capacity, tile), lambda i: (index, 0, i)),
        ]
        + [spec] * len(adds),
        out_specs=spec,
        scratch_shapes=[pltpu.VMEM((rows, capacity), F32)],
        compiler_params=params(1),
        name="combine",
    )(at, block, mine, theirs, *adds)


DEPTH = 4


def send(array, dz=0, dy=0, dc=0, only=None):
    pairs = []
    for z in range(DEPTH):
        if 0 <= z + dz < DEPTH and (only is None or z in only):
            for y in range(2):
                for c in range(2):
                    pairs.append(((z * 2 + y) * 2 + c, ((z + dz) * 2 + (y ^ dy)) * 2 + (c ^ dc)))
    return lax.ppermute(array, "ep", pairs)


def send_far(array):
    pairs = [(i, i + 12) for i in range(4)] + [(i + 12, i) for i in range(4)]
    return lax.ppermute(array, "ep", pairs)


def after(array, *others):
    return lax.optimization_barrier((array,) + others)[0]


def line_shards(tokens, routes, gates, w_gate, w_up, w_down):
    tok_rows, features = tokens.shape
    topk = routes.shape[1]
    experts = lax.axis_size("ep") // 2
    capacity = 2 * ((tok_rows * topk * 5 + 8 * experts - 1) // (8 * experts))
    chip = lax.axis_index("ep") // 2
    at = jnp.stack([chip, chip ^ 1]).astype(jnp.int32)
    own = (w_gate, w_up, w_down)
    other = tuple(send(w, dc=1) for w in own)
    weights = (own, other)

    block, picked = prepare(at, tokens, routes, gates, experts, capacity)
    from_left = send(block, dz=1)
    from_right = send(block, dz=-1)
    picked = send(picked[None], dy=1)
    (near_picked,) = compact(at, (from_left, from_right), experts, capacity)
    near_picked = send(near_picked, dy=1)
    mid_left = send(from_left, dz=1)
    mid_right = send(from_right, dz=-1)
    mid_picked, mid = compact(at, (mid_left, mid_right), experts, capacity, sums=True)
    mid_picked = send(mid_picked, dy=1)
    far = send_far(after(block, mid_left, mid_right))
    (far_picked,) = compact(at, (far,), experts, capacity)
    far_picked = send(far_picked, dy=1)

    own_out, left_out, right_out, own_back, near_back = run_expert(
        at, (block, from_left, from_right), (picked, near_picked), weights, experts
    )
    mid_out, far_out, mid_back, far_back = run_expert(
        at, (mid, far), (mid_picked, far_picked), weights, experts
    )
    near_back = send(near_back, dy=1)
    far_back = send(far_back, dy=1)
    mid_back = send(mid_back, dy=1)
    own_back = send(after(own_back, mid_back, far_back), dy=1)

    far_sum = combine(at, far, far_out, far_back, 0, (), experts)
    far_home = send_far(far_sum)
    mid_sum = combine(at, mid, mid_out, mid_back, 0, (), experts)
    to_right = send(mid_sum, dz=1, only=(0, 1))
    to_left = send(mid_sum, dz=-1, only=(3, 2))
    right_sum = combine(at, from_right, right_out, near_back, 1, (to_right,), experts)
    left_sum = combine(at, from_left, left_out, near_back, 0, (to_left,), experts)
    home_left = send(right_sum, dz=1)
    home_right = send(left_sum, dz=-1)
    return combine(
        at, block, own_out, own_back, 0, (far_home, home_left, home_right), experts
    )


def partner(shard, axis, stride):
    return lax.ppermute(shard, axis, [(i, i ^ 1 << stride) for i in range(lax.axis_size(axis))])


def plain_to_grid(values):
    magnitude = jnp.abs(values)
    spacing = jnp.full(values.shape, 2.0 ** (-9), jnp.float32)
    for exponent in range(-5, 9):
        spacing = jnp.where(magnitude >= 2.0**exponent, spacing * 2.0, spacing)
    grid_value = jnp.floor(magnitude / spacing + 0.5) * spacing
    return jnp.where(values < 0, -grid_value, grid_value)


def quantize(rows):
    row_count = rows.shape[0]
    feature_count = rows.shape[1]
    blocks = rows.astype(jnp.float32).reshape(row_count, feature_count // 128, 128)
    largest = jnp.max(jnp.abs(blocks), axis=2)
    scales = ((largest + 1e-06) / 448.0).astype(jnp.bfloat16)
    scales = lax.optimization_barrier(scales)
    quantized = plain_to_grid(blocks / scales.astype(jnp.float32)[:, :, None]).astype(jnp.bfloat16)
    return (quantized.reshape(row_count, feature_count), scales)


def half_expert(quantized, scales, weights):
    row_count = quantized.shape[0]
    feature_count = quantized.shape[1]
    blocks = quantized.astype(jnp.float32).reshape(row_count, feature_count // 128, 128)
    restored = (blocks * scales.astype(jnp.float32)[:, :, None]).astype(jnp.bfloat16)
    restored = restored.reshape(row_count, feature_count)
    gate_part = jnp.dot(restored, weights[0], preferred_element_type=jnp.float32)
    up_part = jnp.dot(restored, weights[1], preferred_element_type=jnp.float32)
    hidden = (jax.nn.silu(gate_part) * up_part).astype(jnp.bfloat16)
    return jnp.dot(hidden, weights[2], preferred_element_type=jnp.float32)


def plain_expert(quantized, scales, weights):
    return half_expert(quantized, scales, weights)


def shards(tokens, routes, gates, w_gate, w_up, w_down):
    tok_rows, feature_count = tokens.shape
    topk_count = routes.shape[1]
    slices = lax.axis_size("ep")
    experts = slices // 2
    capacity = 2 * ((tok_rows * topk_count * 5 + 8 * experts - 1) // (8 * experts))
    weights = (w_gate[0], w_up[0], w_down[0])
    quantized, scales = quantize(tokens)
    qblocks = scales.shape[1]
    flat_experts = routes.reshape(-1)
    onehot = (flat_experts[:, None] == jnp.arange(experts, dtype=jnp.int32)[None, :]).astype(
        jnp.int32
    )
    rank = jnp.sum((jnp.cumsum(onehot, axis=0) - onehot) * onehot, axis=1)
    slot_index = flat_experts * capacity + rank
    token_of = jnp.arange(tok_rows * topk_count, dtype=jnp.int32) // topk_count
    table = jnp.full((experts * capacity,), tok_rows, jnp.int32).at[slot_index].set(token_of)
    padded_q = jnp.concatenate([quantized, jnp.zeros((1, feature_count), jnp.bfloat16)], axis=0)
    padded_s = jnp.concatenate([scales, jnp.zeros((1, qblocks), jnp.bfloat16)], axis=0)
    send_q = padded_q[table].reshape(experts, capacity, feature_count)
    send_s = padded_s[table].reshape(experts, capacity, qblocks)
    half_slots = capacity // 2
    split_q = send_q.reshape(slices, half_slots, feature_count)
    split_s = send_s.reshape(slices, half_slots, qblocks)
    mine_q, mine_s = (
        lax.all_to_all(split_q, "ep", split_axis=0, concat_axis=0, tiled=True),
        lax.all_to_all(split_s, "ep", split_axis=0, concat_axis=0, tiled=True),
    )
    other_q, other_s = partner((mine_q, mine_s), "ep", 0)
    leading = lax.axis_index("ep") % 2 == 0
    low_q = jnp.where(leading, mine_q, other_q)
    high_q = jnp.where(leading, other_q, mine_q)
    low_s = jnp.where(leading, mine_s, other_s)
    high_s = jnp.where(leading, other_s, mine_s)
    rows_q = jnp.concatenate([low_q, high_q], axis=1)
    rows_s = jnp.concatenate([low_s, high_s], axis=1)
    senders = rows_q.shape[0]
    partial_value = plain_expert(
        rows_q.reshape(senders * capacity, feature_count),
        rows_s.reshape(senders * capacity, qblocks),
        weights,
    )
    rounded = partial_value.astype(jnp.bfloat16).reshape(senders, capacity, feature_count)
    low_part = rounded[:, :half_slots]
    high_part = rounded[:, half_slots:]
    kept_half = jnp.where(leading, low_part, high_part)
    given_half = jnp.where(leading, high_part, low_part)
    partner_sum = partner(given_half, "ep", 0)
    kept_half = lax.optimization_barrier(kept_half)
    summed = (kept_half.astype(jnp.float32) + partner_sum.astype(jnp.float32)).astype(jnp.bfloat16)
    back = lax.all_to_all(summed, "ep", split_axis=0, concat_axis=0, tiled=True)
    expert_out = back.reshape(experts, capacity, feature_count)
    expert_out = lax.optimization_barrier(expert_out).reshape(experts * capacity, feature_count)
    picked = expert_out[slot_index].reshape(tok_rows, topk_count, feature_count)
    mixed = jnp.einsum("tk,tkd->td", gates, picked.astype(jnp.float32))
    return mixed.astype(jnp.bfloat16)


def solution(mesh):
    placed = (
        P(("groups", "ep"), None),
        P(("groups", "ep"), None),
        P(("groups", "ep"), None),
        P("ep", None, None),
        P("ep", None, None),
        P("ep", None, None),
    )
    line = mesh.shape["ep"] == 4 * DEPTH
    return jax.shard_map(
        line_shards if line else shards, mesh=mesh, in_specs=placed, out_specs=P(("groups", "ep"), None), check_vma=False
    )
```

```python
import functools

import jax
import jax.numpy as jnp
from jax import lax
from jax.experimental import pallas as pl
from jax.experimental.pallas import tpu as pltpu
from jax.sharding import PartitionSpec as P

F32 = jnp.float32
BF16 = jnp.bfloat16
LANES = 128
BLOCK = 128
MIB = 1024 * 1024


def params(limit, grid_dims=0):
    semantics = ("arbitrary",) * grid_dims if grid_dims else None
    return pltpu.CompilerParams(vmem_limit_bytes=limit * MIB, dimension_semantics=semantics)


SMEM = pl.BlockSpec(memory_space=pltpu.SMEM)
VMEM = pl.BlockSpec(memory_space=pltpu.VMEM)
ANY = pl.BlockSpec(memory_space=pl.ANY)


def to_grid(values):
    scaled = jnp.abs(values) * 512.0
    above = scaled >= 2.0**11
    power = jnp.where(above, 2.0**-1, 2.0**-9)
    scaled = jnp.where(above, scaled * 2.0**-8, scaled)
    for exponent in (4, 2, 1):
        above = scaled >= 2.0 ** (3 + exponent)
        power = jnp.where(above, power * 2.0**exponent, power)
        scaled = jnp.where(above, scaled * 2.0**-exponent, scaled)
    grid_value = jnp.floor(scaled + 0.5) * power
    return jnp.where(values < 0, -grid_value, grid_value)


def gate_of(ext, expert, experts):
    lane = lax.broadcasted_iota(jnp.int32, ext.shape, 1)
    mine = (lane == expert) | (lane == expert + experts) | (lane == expert + 2 * experts)
    return jnp.sum(jnp.where(mine, ext.astype(F32), 0.0), axis=1, keepdims=True)


def placement(gate):
    rows = gate.shape[0]
    routed = gate > 0.0
    before = lax.broadcasted_iota(jnp.int32, (rows, rows), 1) < lax.broadcasted_iota(
        jnp.int32, (rows, rows), 0
    )
    ones = jnp.broadcast_to(jnp.where(routed, 1.0, 0.0), (rows, LANES)).astype(BF16)
    rank = jnp.dot(jnp.where(before, 1.0, 0.0).astype(BF16), ones, preferred_element_type=F32)
    place = lax.broadcasted_iota(jnp.int32, (rows, LANES), 1)
    return jnp.where(routed & (rank.astype(jnp.int32) == place), 1.0, 0.0)


def picker(gate, capacity):
    return placement(gate).T[:capacity].astype(BF16)


def pick_rows(onehot, rows):
    return jnp.dot(onehot, rows, preferred_element_type=F32).astype(BF16)


def prepare_kernel(experts, capacity, at_ref, tokens_ref, routes_ref, gates_ref, x_ref, y_ref):
    rows, features = tokens_ref.shape
    sub = lax.broadcasted_iota(jnp.int32, (LANES, rows), 0)
    value = jnp.zeros((LANES, rows), F32)
    for k in range(routes_ref.shape[0]):
        route = routes_ref[k : k + 1, :]
        hit = (sub == route) | (sub == route + experts) | (sub == route + 2 * experts)
        value = value + jnp.where(hit, gates_ref[k : k + 1, :], 0.0)
    value = value.T
    lane = lax.broadcasted_iota(jnp.int32, (rows, LANES), 1)
    high = value.astype(BF16).astype(F32)
    middle = (value - high).astype(BF16).astype(F32)
    low = value - high - middle
    ext = jnp.where(lane < experts, high, jnp.where(lane < 2 * experts, middle, low)).astype(BF16)
    onehot = picker(gate_of(ext, at_ref[1], experts), capacity)
    x_ref[:, features:] = ext
    y_ref[:, features:] = pick_rows(onehot, ext)
    step = 4 * BLOCK

    def body(i, carry):
        start = pl.multiple_of(i * step, step)
        tokens = tokens_ref[:, pl.ds(start, step)].astype(F32)
        parts = []
        for b in range(step // BLOCK):
            block = tokens[:, b * BLOCK : (b + 1) * BLOCK]
            largest = jnp.max(jnp.abs(block), axis=1, keepdims=True)
            scale = ((largest + 1e-06) / 448.0).astype(BF16).astype(F32)
            parts.append((to_grid(block / scale) * scale).astype(BF16))
        restored = jnp.concatenate(parts, axis=1)
        x_ref[:, pl.ds(start, step)] = restored
        y_ref[:, pl.ds(start, step)] = pick_rows(onehot, restored)
        return carry

    lax.fori_loop(0, features // step, body, 0, unroll=2)


def prepare(at, tokens, routes, gates, experts, capacity):
    rows, features = tokens.shape
    width = features + LANES
    return pl.pallas_call(
        functools.partial(prepare_kernel, experts, capacity),
        out_shape=(
            jax.ShapeDtypeStruct((rows, width), BF16),
            jax.ShapeDtypeStruct((capacity, width), BF16),
        ),
        in_specs=[SMEM] + [VMEM] * 3,
        out_specs=(VMEM,) * 2,
        compiler_params=params(12),
        name="prepare",
    )(at, tokens, routes.T, gates.T)


def compact_kernel(experts, capacity, count, sums, at_ref, *refs):
    ins, outs = refs[:count], refs[len(refs) - (2 if sums else 1) :]
    features = ins[0].shape[1] - LANES
    step = 1024
    for j in range(1 if sums else count):

        def load(columns, j=j):
            if not sums:
                return ins[j][:, columns]
            merged = ins[0][:, columns] + ins[1][:, columns]
            outs[1][:, columns] = merged
            return merged

        tail = slice(features, features + LANES)
        ext = load(tail)
        onehot = picker(gate_of(ext, at_ref[1], experts), capacity)
        outs[0][j, :, tail] = pick_rows(onehot, ext)
        for start in range(0, features, step):
            columns = slice(start, start + step)
            outs[0][j, :, columns] = pick_rows(onehot, load(columns))


def compact(at, blocks, experts, capacity, sums=False, behind=()):
    rows, width = blocks[0].shape
    count = len(blocks)
    out_shape = [jax.ShapeDtypeStruct((1 if sums else count, capacity, width), BF16)]
    if sums:
        out_shape.append(jax.ShapeDtypeStruct((rows, width), BF16))
    return pl.pallas_call(
        functools.partial(compact_kernel, experts, capacity, count, sums),
        out_shape=tuple(out_shape),
        in_specs=[SMEM] + [VMEM] * count + [ANY] * len(behind),
        out_specs=(VMEM,) * len(out_shape),
        compiler_params=params(12),
        name="compact",
    )(at, *blocks, *behind)


def expert_kernel(experts, full, extra, k_steps, at_ref, *refs):
    count = len(full) + len(extra)
    rows_in, refs = refs[:count], refs[count:]
    exts, refs = refs[:count], refs[count:]
    gate_own, gate_other, up_own, up_other, down_own, down_other = refs[:6]
    outs, (acc, hidden, weight) = refs[len(refs) - 3 - count : -3], refs[-3:]
    i = pl.program_id(0)
    half = gate_own.shape[2]
    pieces = []
    for j, size in enumerate(full):
        pieces.append((j, None, size))
    for j, (blocks, size) in enumerate(extra):
        for b in range(blocks):
            pieces.append((len(full) + j, b, size))

    def load(source, j, b):
        return source[j][...] if b is None else source[j][b]

    @pl.when(i == 0)
    def _():
        acc[...] = jnp.zeros_like(acc)
        weight[...] = jnp.concatenate(
            [
                jnp.broadcast_to(gate_of(load(exts, j, b), at_ref[0], experts), (size, LANES))
                for j, b, size in pieces
            ],
            axis=0,
        )

    @pl.when(i < k_steps)
    def _():
        x = jnp.concatenate([load(rows_in, j, b).astype(F32) for j, b, _ in pieces], axis=0)
        x = x.astype(BF16)
        for n, ref in enumerate((gate_own, gate_other, up_own, up_other)):
            acc[:, n * half : (n + 1) * half] += jnp.dot(x, ref[0], preferred_element_type=F32)

    @pl.when(i == k_steps - 1)
    def _():
        gate_part = acc[:, : 2 * half]
        hidden[...] = (jax.nn.silu(gate_part) * acc[:, 2 * half :]).astype(BF16)

    @pl.when(i >= k_steps)
    def _():
        own = jnp.dot(hidden[:, :half], down_own[0], preferred_element_type=F32)
        other = jnp.dot(hidden[:, half:], down_other[0], preferred_element_type=F32)
        total = own.astype(BF16).astype(F32) + other.astype(BF16).astype(F32)
        scaled = total.astype(BF16).astype(F32) * weight[:, :1]
        offset = 0
        for j, b, size in pieces:
            part = scaled[offset : offset + size].astype(BF16)
            if b is None:
                outs[j][...] = part
            else:
                outs[j][b] = part
            offset += size


def run_expert(at, full, extra, weights, experts, behind=(), tile=1792):
    own, other = weights
    features, half = own[0].shape[1:]
    k_steps = features // tile
    n_steps = features // tile
    last = features // LANES
    inputs = list(full) + list(extra)
    row_specs, ext_specs, out_specs, out_shape = [], [], [], []
    for array in inputs:
        lead = array.shape[:-1]
        zeros = (0,) * len(lead)
        row_specs.append(
            pl.BlockSpec(lead + (tile,), lambda i, z=zeros: z + (jnp.minimum(i, k_steps - 1),))
        )
        ext_specs.append(pl.BlockSpec(lead + (LANES,), lambda i, z=zeros: z + (last,)))
        out_specs.append(
            pl.BlockSpec(lead + (tile,), lambda i, z=zeros: z + (jnp.maximum(i - k_steps, 0),))
        )
        out_shape.append(jax.ShapeDtypeStruct(lead + (features,), BF16))
    up_spec = pl.BlockSpec((1, tile, half), lambda i: (0, jnp.minimum(i, k_steps - 1), 0))
    down_spec = pl.BlockSpec((1, half, tile), lambda i: (0, 0, jnp.maximum(i - k_steps, 0)))
    total = sum(a.size // a.shape[-1] for a in inputs)
    return pl.pallas_call(
        functools.partial(
            expert_kernel,
            experts,
            tuple(a.shape[0] for a in full),
            tuple(a.shape[:2] for a in extra),
            k_steps,
        ),
        out_shape=tuple(out_shape),
        grid=(k_steps + n_steps,),
        in_specs=[SMEM] + row_specs + ext_specs + [up_spec] * 4 + [down_spec] * 2
        + [ANY] * len(behind),
        out_specs=tuple(out_specs),
        scratch_shapes=[
            pltpu.VMEM((total, 4 * half), F32),
            pltpu.VMEM((total, 2 * half), BF16),
            pltpu.VMEM((total, LANES), F32),
        ],
        compiler_params=params(44, 1),
        cost_estimate=pl.CostEstimate(
            flops=12 * total * features * half,
            bytes_accessed=12 * features * half + 4 * total * features,
            transcendentals=2 * total * half,
        ),
        name="expert",
    )(at, *inputs, *inputs, own[0], other[0], own[1], other[1], own[2], other[2], *behind)


def combine_kernel(experts, capacity, index, adds, at_ref, block_ref, mine_ref, theirs_ref, *refs):
    out_ref = refs[-1]
    features = mine_ref.shape[1]
    onehot = placement(gate_of(block_ref[:, features:], at_ref[1], experts))
    onehot = onehot[:, :capacity].astype(BF16)
    step = 1024
    for start in range(0, features, step):
        columns = slice(start, start + step)
        total = mine_ref[:, columns].astype(F32) + jnp.dot(
            onehot, theirs_ref[index, :, columns], preferred_element_type=F32
        )
        for ref in refs[:adds]:
            total = total + ref[:, columns].astype(F32)
        out_ref[:, columns] = total.astype(BF16)


def combine(at, block, mine, theirs, index, adds, experts, behind=()):
    rows, features = mine.shape
    capacity = theirs.shape[1]
    return pl.pallas_call(
        functools.partial(combine_kernel, experts, capacity, index, len(adds)),
        out_shape=jax.ShapeDtypeStruct((rows, features), BF16),
        in_specs=[SMEM] + [VMEM] * (3 + len(adds)) + [ANY] * len(behind),
        out_specs=VMEM,
        compiler_params=params(14),
        name="combine",
    )(at, block, mine, theirs, *adds, *behind)


DEPTH = 4


def send(array, dz=0, dy=0, dc=0, only=None):
    pairs = []
    for z in range(DEPTH):
        if 0 <= z + dz < DEPTH and (only is None or z in only):
            for y in range(2):
                for c in range(2):
                    pairs.append(((z * 2 + y) * 2 + c, ((z + dz) * 2 + (y ^ dy)) * 2 + (c ^ dc)))
    return lax.ppermute(array, "ep", pairs)


def send_far(array):
    pairs = [(i, i + 12) for i in range(4)] + [(i + 12, i) for i in range(4)]
    return lax.ppermute(array, "ep", pairs)


def after(array, *others):
    return lax.optimization_barrier((array,) + others)[0]


def line_shards(tokens, routes, gates, w_gate, w_up, w_down):
    tok_rows, features = tokens.shape
    topk = routes.shape[1]
    experts = lax.axis_size("ep") // 2
    capacity = 2 * ((tok_rows * topk * 5 + 8 * experts - 1) // (8 * experts))
    chip = lax.axis_index("ep") // 2
    at = jnp.stack([chip, chip ^ 1]).astype(jnp.int32)
    own = (w_gate, w_up, w_down)
    other = tuple(send(w, dc=1) for w in own)
    weights = (own, other)

    block, picked = prepare(at, tokens, routes, gates, experts, capacity)
    from_left = send(block, dz=1)
    from_right = send(block, dz=-1)
    picked = send(picked[None], dy=1)
    mid_left = send(after(from_left, from_right), dz=1)
    mid_right = send(after(from_right, from_left), dz=-1)
    (near_picked,) = compact(at, (from_left, from_right), experts, capacity, behind=(picked,))
    far = send_far(after(block, mid_left, mid_right, near_picked))
    near_picked = send(near_picked, dy=1)
    mid_picked, mid = compact(at, (mid_left, mid_right), experts, capacity, sums=True)
    mid_picked = send(mid_picked, dy=1)
    own_out, left_out, right_out, own_back, near_back = run_expert(
        at, (block, from_left, from_right), (picked, near_picked), weights, experts
    )
    (far_picked,) = compact(at, (far,), experts, capacity)
    far_picked = send(far_picked, dy=1)
    mid_out, far_out, mid_back, far_back = run_expert(
        at, (mid, far), (mid_picked, far_picked), weights, experts, behind=(near_back,)
    )
    near_back = send(near_back, dy=1)
    mid_back = send(after(mid_back, near_back), dy=1)
    far_back = send(after(far_back, mid_back), dy=1)
    own_back = send(after(own_back, far_back), dy=1)

    mid_sum = combine(at, mid, mid_out, mid_back, 0, (), experts)
    to_right = send(mid_sum, dz=1, only=(0, 1))
    to_left = send(mid_sum, dz=-1, only=(3, 2))
    far_sum = combine(at, far, far_out, far_back, 0, (), experts, behind=(mid_sum,))
    far_home = send_far(far_sum)
    right_sum = combine(at, from_right, right_out, near_back, 1, (to_right,), experts)
    left_sum = combine(at, from_left, left_out, near_back, 0, (to_left,), experts)
    home_left = send(right_sum, dz=1)
    home_right = send(left_sum, dz=-1)
    return combine(at, block, own_out, own_back, 0, (far_home, home_left, home_right), experts)


def partner(shard, axis, stride):
    return lax.ppermute(shard, axis, [(i, i ^ 1 << stride) for i in range(lax.axis_size(axis))])


def plain_to_grid(values):
    magnitude = jnp.abs(values)
    spacing = jnp.full(values.shape, 2.0 ** (-9), jnp.float32)
    for exponent in range(-5, 9):
        spacing = jnp.where(magnitude >= 2.0**exponent, spacing * 2.0, spacing)
    grid_value = jnp.floor(magnitude / spacing + 0.5) * spacing
    return jnp.where(values < 0, -grid_value, grid_value)


def quantize(rows):
    row_count = rows.shape[0]
    feature_count = rows.shape[1]
    blocks = rows.astype(jnp.float32).reshape(row_count, feature_count // 128, 128)
    largest = jnp.max(jnp.abs(blocks), axis=2)
    scales = ((largest + 1e-06) / 448.0).astype(jnp.bfloat16)
    scales = lax.optimization_barrier(scales)
    quantized = plain_to_grid(blocks / scales.astype(jnp.float32)[:, :, None]).astype(jnp.bfloat16)
    return (quantized.reshape(row_count, feature_count), scales)


def half_expert(quantized, scales, weights):
    row_count = quantized.shape[0]
    feature_count = quantized.shape[1]
    blocks = quantized.astype(jnp.float32).reshape(row_count, feature_count // 128, 128)
    restored = (blocks * scales.astype(jnp.float32)[:, :, None]).astype(jnp.bfloat16)
    restored = restored.reshape(row_count, feature_count)
    gate_part = jnp.dot(restored, weights[0], preferred_element_type=jnp.float32)
    up_part = jnp.dot(restored, weights[1], preferred_element_type=jnp.float32)
    hidden = (jax.nn.silu(gate_part) * up_part).astype(jnp.bfloat16)
    return jnp.dot(hidden, weights[2], preferred_element_type=jnp.float32)


def plain_expert(quantized, scales, weights):
    return half_expert(quantized, scales, weights)


def shards(tokens, routes, gates, w_gate, w_up, w_down):
    tok_rows, feature_count = tokens.shape
    topk_count = routes.shape[1]
    slices = lax.axis_size("ep")
    experts = slices // 2
    capacity = 2 * ((tok_rows * topk_count * 5 + 8 * experts - 1) // (8 * experts))
    weights = (w_gate[0], w_up[0], w_down[0])
    quantized, scales = quantize(tokens)
    qblocks = scales.shape[1]
    flat_experts = routes.reshape(-1)
    onehot = (flat_experts[:, None] == jnp.arange(experts, dtype=jnp.int32)[None, :]).astype(
        jnp.int32
    )
    rank = jnp.sum((jnp.cumsum(onehot, axis=0) - onehot) * onehot, axis=1)
    slot_index = flat_experts * capacity + rank
    token_of = jnp.arange(tok_rows * topk_count, dtype=jnp.int32) // topk_count
    table = jnp.full((experts * capacity,), tok_rows, jnp.int32).at[slot_index].set(token_of)
    padded_q = jnp.concatenate([quantized, jnp.zeros((1, feature_count), jnp.bfloat16)], axis=0)
    padded_s = jnp.concatenate([scales, jnp.zeros((1, qblocks), jnp.bfloat16)], axis=0)
    send_q = padded_q[table].reshape(experts, capacity, feature_count)
    send_s = padded_s[table].reshape(experts, capacity, qblocks)
    half_slots = capacity // 2
    split_q = send_q.reshape(slices, half_slots, feature_count)
    split_s = send_s.reshape(slices, half_slots, qblocks)
    mine_q, mine_s = (
        lax.all_to_all(split_q, "ep", split_axis=0, concat_axis=0, tiled=True),
        lax.all_to_all(split_s, "ep", split_axis=0, concat_axis=0, tiled=True),
    )
    other_q, other_s = partner((mine_q, mine_s), "ep", 0)
    leading = lax.axis_index("ep") % 2 == 0
    low_q = jnp.where(leading, mine_q, other_q)
    high_q = jnp.where(leading, other_q, mine_q)
    low_s = jnp.where(leading, mine_s, other_s)
    high_s = jnp.where(leading, other_s, mine_s)
    rows_q = jnp.concatenate([low_q, high_q], axis=1)
    rows_s = jnp.concatenate([low_s, high_s], axis=1)
    senders = rows_q.shape[0]
    partial_value = plain_expert(
        rows_q.reshape(senders * capacity, feature_count),
        rows_s.reshape(senders * capacity, qblocks),
        weights,
    )
    rounded = partial_value.astype(jnp.bfloat16).reshape(senders, capacity, feature_count)
    low_part = rounded[:, :half_slots]
    high_part = rounded[:, half_slots:]
    kept_half = jnp.where(leading, low_part, high_part)
    given_half = jnp.where(leading, high_part, low_part)
    partner_sum = partner(given_half, "ep", 0)
    kept_half = lax.optimization_barrier(kept_half)
    summed = (kept_half.astype(jnp.float32) + partner_sum.astype(jnp.float32)).astype(jnp.bfloat16)
    back = lax.all_to_all(summed, "ep", split_axis=0, concat_axis=0, tiled=True)
    expert_out = back.reshape(experts, capacity, feature_count)
    expert_out = lax.optimization_barrier(expert_out).reshape(experts * capacity, feature_count)
    picked = expert_out[slot_index].reshape(tok_rows, topk_count, feature_count)
    mixed = jnp.einsum("tk,tkd->td", gates, picked.astype(jnp.float32))
    return mixed.astype(jnp.bfloat16)


def solution(mesh):
    placed = (
        P(("groups", "ep"), None),
        P(("groups", "ep"), None),
        P(("groups", "ep"), None),
        P("ep", None, None),
        P("ep", None, None),
        P("ep", None, None),
    )
    line = mesh.shape["ep"] == 4 * DEPTH
    return jax.shard_map(
        line_shards if line else shards, mesh=mesh, in_specs=placed, out_specs=P(("groups", "ep"), None), check_vma=False
    )
```

```python
import functools

import jax
import jax.numpy as jnp
from jax import lax
from jax.experimental import pallas as pl
from jax.experimental.pallas import tpu as pltpu
from jax.sharding import PartitionSpec as P

F32 = jnp.float32
BF16 = jnp.bfloat16
LANES = 128
BLOCK = 128
MIB = 1024 * 1024
COST = 1024


def params(limit, grid_dims=0):
    semantics = ("arbitrary",) * grid_dims if grid_dims else None
    return pltpu.CompilerParams(vmem_limit_bytes=limit * MIB, dimension_semantics=semantics)


SMEM = pl.BlockSpec(memory_space=pltpu.SMEM)
VMEM = pl.BlockSpec(memory_space=pltpu.VMEM)
ANY = pl.BlockSpec(memory_space=pl.ANY)


def to_grid(values):
    scaled = jnp.abs(values) * 512.0
    above = scaled >= 2.0**11
    power = jnp.where(above, 2.0**-1, 2.0**-9)
    scaled = jnp.where(above, scaled * 2.0**-8, scaled)
    for exponent in (4, 2, 1):
        above = scaled >= 2.0 ** (3 + exponent)
        power = jnp.where(above, power * 2.0**exponent, power)
        scaled = jnp.where(above, scaled * 2.0**-exponent, scaled)
    grid_value = jnp.floor(scaled + 0.5) * power
    return jnp.where(values < 0, -grid_value, grid_value)


def gate_of(ext, expert, experts):
    lane = lax.broadcasted_iota(jnp.int32, ext.shape, 1)
    mine = (lane == expert) | (lane == expert + experts) | (lane == expert + 2 * experts)
    return jnp.sum(jnp.where(mine, ext.astype(F32), 0.0), axis=1, keepdims=True)


def placement(gate):
    rows = gate.shape[0]
    routed = gate > 0.0
    before = lax.broadcasted_iota(jnp.int32, (rows, rows), 1) < lax.broadcasted_iota(
        jnp.int32, (rows, rows), 0
    )
    ones = jnp.broadcast_to(jnp.where(routed, 1.0, 0.0), (rows, LANES)).astype(BF16)
    rank = jnp.dot(jnp.where(before, 1.0, 0.0).astype(BF16), ones, preferred_element_type=F32)
    place = lax.broadcasted_iota(jnp.int32, (rows, LANES), 1)
    return jnp.where(routed & (rank.astype(jnp.int32) == place), 1.0, 0.0)


def picker(gate, capacity):
    return placement(gate).T[:capacity].astype(BF16)


def pick_rows(onehot, rows):
    return jnp.dot(onehot, rows, preferred_element_type=F32).astype(BF16)


def prepare_kernel(experts, capacity, at_ref, tokens_ref, routes_ref, gates_ref, x_ref, y_ref):
    rows, features = tokens_ref.shape
    sub = lax.broadcasted_iota(jnp.int32, (LANES, rows), 0)
    value = jnp.zeros((LANES, rows), F32)
    for k in range(routes_ref.shape[0]):
        route = routes_ref[k : k + 1, :]
        hit = (sub == route) | (sub == route + experts) | (sub == route + 2 * experts)
        value = value + jnp.where(hit, gates_ref[k : k + 1, :], 0.0)
    value = value.T
    lane = lax.broadcasted_iota(jnp.int32, (rows, LANES), 1)
    high = value.astype(BF16).astype(F32)
    middle = (value - high).astype(BF16).astype(F32)
    low = value - high - middle
    ext = jnp.where(lane < experts, high, jnp.where(lane < 2 * experts, middle, low)).astype(BF16)
    onehot = picker(gate_of(ext, at_ref[1], experts), capacity)
    x_ref[:, features:] = ext
    y_ref[:, features:] = pick_rows(onehot, ext)
    step = 4 * BLOCK

    def body(i, carry):
        start = pl.multiple_of(i * step, step)
        tokens = tokens_ref[:, pl.ds(start, step)].astype(F32)
        parts = []
        for b in range(step // BLOCK):
            block = tokens[:, b * BLOCK : (b + 1) * BLOCK]
            largest = jnp.max(jnp.abs(block), axis=1, keepdims=True)
            scale = ((largest + 1e-06) / 448.0).astype(BF16).astype(F32)
            parts.append((to_grid(block / scale) * scale).astype(BF16))
        restored = jnp.concatenate(parts, axis=1)
        x_ref[:, pl.ds(start, step)] = restored
        y_ref[:, pl.ds(start, step)] = pick_rows(onehot, restored)
        return carry

    lax.fori_loop(0, features // step, body, 0, unroll=2)


def prepare(at, tokens, routes, gates, experts, capacity):
    rows, features = tokens.shape
    width = features + LANES
    return pl.pallas_call(
        functools.partial(prepare_kernel, experts, capacity),
        out_shape=(
            jax.ShapeDtypeStruct((rows, width), BF16),
            jax.ShapeDtypeStruct((capacity, width), BF16),
        ),
        in_specs=[SMEM] + [VMEM] * 3,
        out_specs=(VMEM,) * 2,
        compiler_params=params(12),
        name="prepare",
    )(at, tokens, routes.T, gates.T)


def compact_kernel(experts, capacity, count, sums, at_ref, *refs):
    ins, outs = refs[:count], refs[len(refs) - (2 if sums else 1) :]
    features = ins[0].shape[1] - LANES
    step = 1024
    for j in range(1 if sums else count):

        def load(columns, j=j):
            if not sums:
                return ins[j][:, columns]
            merged = ins[0][:, columns] + ins[1][:, columns]
            outs[1][:, columns] = merged
            return merged

        tail = slice(features, features + LANES)
        ext = load(tail)
        onehot = picker(gate_of(ext, at_ref[1], experts), capacity)
        outs[0][j, :, tail] = pick_rows(onehot, ext)
        for start in range(0, features, step):
            columns = slice(start, start + step)
            outs[0][j, :, columns] = pick_rows(onehot, load(columns))


def compact(at, blocks, experts, capacity, sums=False, behind=()):
    rows, width = blocks[0].shape
    count = len(blocks)
    out_shape = [jax.ShapeDtypeStruct((1 if sums else count, capacity, width), BF16)]
    if sums:
        out_shape.append(jax.ShapeDtypeStruct((rows, width), BF16))
    return pl.pallas_call(
        functools.partial(compact_kernel, experts, capacity, count, sums),
        out_shape=tuple(out_shape),
        in_specs=[SMEM] + [VMEM] * count + [ANY] * len(behind),
        out_specs=(VMEM,) * len(out_shape),
        compiler_params=params(12),
        name="compact",
    )(at, *blocks, *behind)


def expert_kernel(experts, full, extra, k_steps, at_ref, *refs):
    count = len(full) + len(extra)
    rows_in, refs = refs[:count], refs[count:]
    exts, refs = refs[:count], refs[count:]
    gate_own, gate_other, up_own, up_other, down_own, down_other = refs[:6]
    outs, (acc, hidden, weight) = refs[len(refs) - 3 - count : -3], refs[-3:]
    i = pl.program_id(0)
    half = gate_own.shape[2]
    pieces = []
    for j, size in enumerate(full):
        pieces.append((j, None, size))
    for j, (blocks, size) in enumerate(extra):
        for b in range(blocks):
            pieces.append((len(full) + j, b, size))

    def load(source, j, b):
        return source[j][...] if b is None else source[j][b]

    @pl.when(i == 0)
    def _():
        acc[...] = jnp.zeros_like(acc)
        weight[...] = jnp.concatenate(
            [
                jnp.broadcast_to(gate_of(load(exts, j, b), at_ref[0], experts), (size, LANES))
                for j, b, size in pieces
            ],
            axis=0,
        )

    @pl.when(i < k_steps)
    def _():
        x = jnp.concatenate([load(rows_in, j, b).astype(F32) for j, b, _ in pieces], axis=0)
        x = x.astype(BF16)
        for n, ref in enumerate((gate_own, gate_other, up_own, up_other)):
            acc[:, n * half : (n + 1) * half] += jnp.dot(x, ref[0], preferred_element_type=F32)

    @pl.when(i == k_steps - 1)
    def _():
        gate_part = acc[:, : 2 * half]
        hidden[...] = (jax.nn.silu(gate_part) * acc[:, 2 * half :]).astype(BF16)

    @pl.when(i >= k_steps)
    def _():
        own = jnp.dot(hidden[:, :half], down_own[0], preferred_element_type=F32)
        other = jnp.dot(hidden[:, half:], down_other[0], preferred_element_type=F32)
        total = own.astype(BF16).astype(F32) + other.astype(BF16).astype(F32)
        scaled = total.astype(BF16).astype(F32) * weight[:, :1]
        offset = 0
        for j, b, size in pieces:
            part = scaled[offset : offset + size].astype(BF16)
            if b is None:
                outs[j][...] = part
            else:
                outs[j][b] = part
            offset += size


def run_expert(at, full, extra, weights, experts, behind=(), tile=1792):
    own, other = weights
    features, half = own[0].shape[1:]
    k_steps = features // tile
    n_steps = features // tile
    last = features // LANES
    inputs = list(full) + list(extra)
    row_specs, ext_specs, out_specs, out_shape = [], [], [], []
    for array in inputs:
        lead = array.shape[:-1]
        zeros = (0,) * len(lead)
        row_specs.append(
            pl.BlockSpec(lead + (tile,), lambda i, z=zeros: z + (jnp.minimum(i, k_steps - 1),))
        )
        ext_specs.append(pl.BlockSpec(lead + (LANES,), lambda i, z=zeros: z + (last,)))
        out_specs.append(
            pl.BlockSpec(lead + (tile,), lambda i, z=zeros: z + (jnp.maximum(i - k_steps, 0),))
        )
        out_shape.append(jax.ShapeDtypeStruct(lead + (features,), BF16))
    up_spec = pl.BlockSpec((1, tile, half), lambda i: (0, jnp.minimum(i, k_steps - 1), 0))
    down_spec = pl.BlockSpec((1, half, tile), lambda i: (0, 0, jnp.maximum(i - k_steps, 0)))
    total = sum(a.size // a.shape[-1] for a in inputs)
    return pl.pallas_call(
        functools.partial(
            expert_kernel,
            experts,
            tuple(a.shape[0] for a in full),
            tuple(a.shape[:2] for a in extra),
            k_steps,
        ),
        out_shape=tuple(out_shape),
        grid=(k_steps + n_steps,),
        in_specs=[SMEM] + row_specs + ext_specs + [up_spec] * 4 + [down_spec] * 2
        + [ANY] * len(behind),
        out_specs=tuple(out_specs),
        scratch_shapes=[
            pltpu.VMEM((total, 4 * half), F32),
            pltpu.VMEM((total, 2 * half), BF16),
            pltpu.VMEM((total, LANES), F32),
        ],
        compiler_params=params(44, 1),
        cost_estimate=pl.CostEstimate(flops=COST, bytes_accessed=COST, transcendentals=0),
        name="expert",
    )(at, *inputs, *inputs, own[0], other[0], own[1], other[1], own[2], other[2], *behind)


def combine_kernel(experts, capacity, index, adds, at_ref, block_ref, mine_ref, theirs_ref, *refs):
    out_ref = refs[-1]
    features = mine_ref.shape[1]
    onehot = placement(gate_of(block_ref[:, features:], at_ref[1], experts))
    onehot = onehot[:, :capacity].astype(BF16)
    step = 1024
    for start in range(0, features, step):
        columns = slice(start, start + step)
        total = mine_ref[:, columns].astype(F32) + jnp.dot(
            onehot, theirs_ref[index, :, columns], preferred_element_type=F32
        )
        for ref in refs[:adds]:
            total = total + ref[:, columns].astype(F32)
        out_ref[:, columns] = total.astype(BF16)


def combine(at, block, mine, theirs, index, adds, experts, behind=()):
    rows, features = mine.shape
    capacity = theirs.shape[1]
    return pl.pallas_call(
        functools.partial(combine_kernel, experts, capacity, index, len(adds)),
        out_shape=jax.ShapeDtypeStruct((rows, features), BF16),
        in_specs=[SMEM] + [VMEM] * (3 + len(adds)) + [ANY] * len(behind),
        out_specs=VMEM,
        compiler_params=params(14),
        name="combine",
    )(at, block, mine, theirs, *adds, *behind)


DEPTH = 4


def send(array, dz=0, dy=0, dc=0, only=None):
    pairs = []
    for z in range(DEPTH):
        if 0 <= z + dz < DEPTH and (only is None or z in only):
            for y in range(2):
                for c in range(2):
                    pairs.append(((z * 2 + y) * 2 + c, ((z + dz) * 2 + (y ^ dy)) * 2 + (c ^ dc)))
    return lax.ppermute(array, "ep", pairs)


def send_far(array):
    pairs = [(i, i + 12) for i in range(4)] + [(i + 12, i) for i in range(4)]
    return lax.ppermute(array, "ep", pairs)


def after(array, *others):
    return lax.optimization_barrier((array,) + others)[0]


def line_shards(tokens, routes, gates, w_gate, w_up, w_down):
    tok_rows, features = tokens.shape
    topk = routes.shape[1]
    experts = lax.axis_size("ep") // 2
    capacity = 2 * ((tok_rows * topk * 5 + 8 * experts - 1) // (8 * experts))
    chip = lax.axis_index("ep") // 2
    at = jnp.stack([chip, chip ^ 1]).astype(jnp.int32)
    block, picked = prepare(at, tokens, routes, gates, experts, capacity)
    other_gate, other_up = send(w_gate, dc=1), send(w_up, dc=1)
    from_left = send(block, dz=1)
    from_right = send(block, dz=-1)
    picked = send(picked[None], dy=1)

    first = (from_left, from_right, picked, other_gate, other_up)
    from_left, from_right, picked, other_gate, other_up = lax.optimization_barrier(first)
    other_down = send(after(w_down, *first), dc=1)
    mid_left = send(from_left, dz=1)
    mid_right = send(from_right, dz=-1)
    (near_picked,) = compact(at, (from_left, from_right), experts, capacity)
    near_picked = send(near_picked, dy=1)

    far = send_far(after(block, mid_left, mid_right, near_picked, other_down))
    mid_picked, mid = compact(at, (mid_left, mid_right), experts, capacity, sums=True)
    mid_picked = send(mid_picked, dy=1)
    weights = ((w_gate, w_up, w_down), (other_gate, other_up, other_down))
    block_out, left_out, right_out, back, near_back = run_expert(
        at, (block, from_left, from_right), (picked, near_picked), weights, experts
    )

    (far_picked,) = compact(at, (far,), experts, capacity, behind=(near_back, mid_picked))
    far_picked = send(far_picked, dy=1)
    mid_out, far_out, mid_back, far_back = run_expert(
        at, (mid, far), (mid_picked, far_picked), weights, experts
    )
    near_back = send(after(near_back, far_picked), dy=1)
    mid_back = send(after(mid_back, near_back), dy=1)
    far_back = send(after(far_back, mid_back), dy=1)
    back = send(after(back, far_back), dy=1)

    mid_sum = combine(at, mid, mid_out, mid_back, 0, (), experts)
    to_right = send(mid_sum, dz=1, only=(0, 1))
    to_left = send(mid_sum, dz=-1, only=(3, 2))
    far_sum = combine(at, far, far_out, far_back, 0, (), experts, behind=(mid_sum,))
    far_home = send_far(far_sum)
    right_sum = combine(at, from_right, right_out, near_back, 1, (to_right,), experts)
    left_sum = combine(at, from_left, left_out, near_back, 0, (to_left,), experts)
    home_left = send(right_sum, dz=1)
    home_right = send(left_sum, dz=-1)
    return combine(at, block, block_out, back, 0, (far_home, home_left, home_right), experts)


def partner(shard, axis, stride):
    return lax.ppermute(shard, axis, [(i, i ^ 1 << stride) for i in range(lax.axis_size(axis))])


def plain_to_grid(values):
    magnitude = jnp.abs(values)
    spacing = jnp.full(values.shape, 2.0 ** (-9), jnp.float32)
    for exponent in range(-5, 9):
        spacing = jnp.where(magnitude >= 2.0**exponent, spacing * 2.0, spacing)
    grid_value = jnp.floor(magnitude / spacing + 0.5) * spacing
    return jnp.where(values < 0, -grid_value, grid_value)


def quantize(rows):
    row_count = rows.shape[0]
    feature_count = rows.shape[1]
    blocks = rows.astype(jnp.float32).reshape(row_count, feature_count // 128, 128)
    largest = jnp.max(jnp.abs(blocks), axis=2)
    scales = ((largest + 1e-06) / 448.0).astype(jnp.bfloat16)
    scales = lax.optimization_barrier(scales)
    quantized = plain_to_grid(blocks / scales.astype(jnp.float32)[:, :, None]).astype(jnp.bfloat16)
    return (quantized.reshape(row_count, feature_count), scales)


def half_expert(quantized, scales, weights):
    row_count = quantized.shape[0]
    feature_count = quantized.shape[1]
    blocks = quantized.astype(jnp.float32).reshape(row_count, feature_count // 128, 128)
    restored = (blocks * scales.astype(jnp.float32)[:, :, None]).astype(jnp.bfloat16)
    restored = restored.reshape(row_count, feature_count)
    gate_part = jnp.dot(restored, weights[0], preferred_element_type=jnp.float32)
    up_part = jnp.dot(restored, weights[1], preferred_element_type=jnp.float32)
    hidden = (jax.nn.silu(gate_part) * up_part).astype(jnp.bfloat16)
    return jnp.dot(hidden, weights[2], preferred_element_type=jnp.float32)


def plain_expert(quantized, scales, weights):
    return half_expert(quantized, scales, weights)


def shards(tokens, routes, gates, w_gate, w_up, w_down):
    tok_rows, feature_count = tokens.shape
    topk_count = routes.shape[1]
    slices = lax.axis_size("ep")
    experts = slices // 2
    capacity = 2 * ((tok_rows * topk_count * 5 + 8 * experts - 1) // (8 * experts))
    weights = (w_gate[0], w_up[0], w_down[0])
    quantized, scales = quantize(tokens)
    qblocks = scales.shape[1]
    flat_experts = routes.reshape(-1)
    onehot = (flat_experts[:, None] == jnp.arange(experts, dtype=jnp.int32)[None, :]).astype(
        jnp.int32
    )
    rank = jnp.sum((jnp.cumsum(onehot, axis=0) - onehot) * onehot, axis=1)
    slot_index = flat_experts * capacity + rank
    token_of = jnp.arange(tok_rows * topk_count, dtype=jnp.int32) // topk_count
    table = jnp.full((experts * capacity,), tok_rows, jnp.int32).at[slot_index].set(token_of)
    padded_q = jnp.concatenate([quantized, jnp.zeros((1, feature_count), jnp.bfloat16)], axis=0)
    padded_s = jnp.concatenate([scales, jnp.zeros((1, qblocks), jnp.bfloat16)], axis=0)
    send_q = padded_q[table].reshape(experts, capacity, feature_count)
    send_s = padded_s[table].reshape(experts, capacity, qblocks)
    half_slots = capacity // 2
    split_q = send_q.reshape(slices, half_slots, feature_count)
    split_s = send_s.reshape(slices, half_slots, qblocks)
    mine_q, mine_s = (
        lax.all_to_all(split_q, "ep", split_axis=0, concat_axis=0, tiled=True),
        lax.all_to_all(split_s, "ep", split_axis=0, concat_axis=0, tiled=True),
    )
    other_q, other_s = partner((mine_q, mine_s), "ep", 0)
    leading = lax.axis_index("ep") % 2 == 0
    low_q = jnp.where(leading, mine_q, other_q)
    high_q = jnp.where(leading, other_q, mine_q)
    low_s = jnp.where(leading, mine_s, other_s)
    high_s = jnp.where(leading, other_s, mine_s)
    rows_q = jnp.concatenate([low_q, high_q], axis=1)
    rows_s = jnp.concatenate([low_s, high_s], axis=1)
    senders = rows_q.shape[0]
    partial_value = plain_expert(
        rows_q.reshape(senders * capacity, feature_count),
        rows_s.reshape(senders * capacity, qblocks),
        weights,
    )
    rounded = partial_value.astype(jnp.bfloat16).reshape(senders, capacity, feature_count)
    low_part = rounded[:, :half_slots]
    high_part = rounded[:, half_slots:]
    kept_half = jnp.where(leading, low_part, high_part)
    given_half = jnp.where(leading, high_part, low_part)
    partner_sum = partner(given_half, "ep", 0)
    kept_half = lax.optimization_barrier(kept_half)
    summed = (kept_half.astype(jnp.float32) + partner_sum.astype(jnp.float32)).astype(jnp.bfloat16)
    back = lax.all_to_all(summed, "ep", split_axis=0, concat_axis=0, tiled=True)
    expert_out = back.reshape(experts, capacity, feature_count)
    expert_out = lax.optimization_barrier(expert_out).reshape(experts * capacity, feature_count)
    picked = expert_out[slot_index].reshape(tok_rows, topk_count, feature_count)
    mixed = jnp.einsum("tk,tkd->td", gates, picked.astype(jnp.float32))
    return mixed.astype(jnp.bfloat16)


def solution(mesh):
    placed = (
        P(("groups", "ep"), None),
        P(("groups", "ep"), None),
        P(("groups", "ep"), None),
        P("ep", None, None),
        P("ep", None, None),
        P("ep", None, None),
    )
    line = mesh.shape["ep"] == 4 * DEPTH
    return jax.shard_map(
        line_shards if line else shards, mesh=mesh, in_specs=placed, out_specs=P(("groups", "ep"), None), check_vma=False
    )
```

```python
import functools

import jax
import jax.numpy as jnp
from jax import lax
from jax.experimental import pallas as pl
from jax.experimental.pallas import tpu as pltpu
from jax.sharding import PartitionSpec as P

F32 = jnp.float32
BF16 = jnp.bfloat16
LANES = 128
BLOCK = 128
MIB = 1024 * 1024
COST = 1024


def params(limit, grid_dims=0):
    semantics = ("arbitrary",) * grid_dims if grid_dims else None
    return pltpu.CompilerParams(vmem_limit_bytes=limit * MIB, dimension_semantics=semantics)


SMEM = pl.BlockSpec(memory_space=pltpu.SMEM)
VMEM = pl.BlockSpec(memory_space=pltpu.VMEM)
ANY = pl.BlockSpec(memory_space=pl.ANY)


def to_grid(values):
    scaled = jnp.abs(values) * 512.0
    above = scaled >= 2.0**11
    power = jnp.where(above, 2.0**-1, 2.0**-9)
    scaled = jnp.where(above, scaled * 2.0**-8, scaled)
    for exponent in (4, 2, 1):
        above = scaled >= 2.0 ** (3 + exponent)
        power = jnp.where(above, power * 2.0**exponent, power)
        scaled = jnp.where(above, scaled * 2.0**-exponent, scaled)
    grid_value = jnp.floor(scaled + 0.5) * power
    return jnp.where(values < 0, -grid_value, grid_value)


def gate_of(ext, expert, experts):
    lane = lax.broadcasted_iota(jnp.int32, ext.shape, 1)
    mine = (lane == expert) | (lane == expert + experts) | (lane == expert + 2 * experts)
    return jnp.sum(jnp.where(mine, ext.astype(F32), 0.0), axis=1, keepdims=True)


def placement(gate):
    rows = gate.shape[0]
    routed = gate > 0.0
    before = lax.broadcasted_iota(jnp.int32, (rows, rows), 1) < lax.broadcasted_iota(
        jnp.int32, (rows, rows), 0
    )
    ones = jnp.broadcast_to(jnp.where(routed, 1.0, 0.0), (rows, LANES)).astype(BF16)
    rank = jnp.dot(jnp.where(before, 1.0, 0.0).astype(BF16), ones, preferred_element_type=F32)
    place = lax.broadcasted_iota(jnp.int32, (rows, LANES), 1)
    return jnp.where(routed & (rank.astype(jnp.int32) == place), 1.0, 0.0)


def picker(gate, capacity):
    return placement(gate).T[:capacity].astype(BF16)


def pick_rows(onehot, rows):
    return jnp.dot(onehot, rows, preferred_element_type=F32).astype(BF16)


def prepare_kernel(experts, capacity, at_ref, tokens_ref, routes_ref, gates_ref, x_ref, y_ref):
    rows, features = tokens_ref.shape
    sub = lax.broadcasted_iota(jnp.int32, (LANES, rows), 0)
    value = jnp.zeros((LANES, rows), F32)
    for k in range(routes_ref.shape[0]):
        route = routes_ref[k : k + 1, :]
        hit = (sub == route) | (sub == route + experts) | (sub == route + 2 * experts)
        value = value + jnp.where(hit, gates_ref[k : k + 1, :], 0.0)
    value = value.T
    lane = lax.broadcasted_iota(jnp.int32, (rows, LANES), 1)
    high = value.astype(BF16).astype(F32)
    middle = (value - high).astype(BF16).astype(F32)
    low = value - high - middle
    ext = jnp.where(lane < experts, high, jnp.where(lane < 2 * experts, middle, low)).astype(BF16)
    onehot = picker(gate_of(ext, at_ref[1], experts), capacity)
    x_ref[:, features:] = ext
    y_ref[:, features:] = pick_rows(onehot, ext)
    step = 4 * BLOCK

    def body(i, carry):
        start = pl.multiple_of(i * step, step)
        tokens = tokens_ref[:, pl.ds(start, step)].astype(F32)
        parts = []
        for b in range(step // BLOCK):
            block = tokens[:, b * BLOCK : (b + 1) * BLOCK]
            largest = jnp.max(jnp.abs(block), axis=1, keepdims=True)
            scale = ((largest + 1e-06) / 448.0).astype(BF16).astype(F32)
            parts.append((to_grid(block / scale) * scale).astype(BF16))
        restored = jnp.concatenate(parts, axis=1)
        x_ref[:, pl.ds(start, step)] = restored
        y_ref[:, pl.ds(start, step)] = pick_rows(onehot, restored)
        return carry

    lax.fori_loop(0, features // step, body, 0, unroll=2)


def prepare(at, tokens, routes, gates, experts, capacity):
    rows, features = tokens.shape
    width = features + LANES
    return pl.pallas_call(
        functools.partial(prepare_kernel, experts, capacity),
        out_shape=(
            jax.ShapeDtypeStruct((rows, width), BF16),
            jax.ShapeDtypeStruct((capacity, width), BF16),
        ),
        in_specs=[SMEM] + [VMEM] * 3,
        out_specs=(VMEM,) * 2,
        compiler_params=params(12),
        name="prepare",
    )(at, tokens, routes.T, gates.T)


def compact_kernel(experts, capacity, choice, at_ref, first_ref, second_ref, *refs):
    picked_ref, block_ref = refs[-2:]
    features = first_ref.shape[1] - LANES
    use_first = at_ref[choice] == 1

    @pl.when(use_first)
    def _():
        block_ref[...] = first_ref[...]

    @pl.when(jnp.logical_not(use_first))
    def _():
        block_ref[...] = second_ref[...]

    ext = block_ref[:, features:]
    onehot = picker(gate_of(ext, at_ref[1], experts), capacity)
    picked_ref[0, :, features:] = pick_rows(onehot, ext)
    step = 1024
    for start in range(0, features, step):
        columns = slice(start, start + step)
        picked_ref[0, :, columns] = pick_rows(onehot, block_ref[:, columns])


def compact(at, choice, first, second, experts, capacity, behind=()):
    rows, width = first.shape
    return pl.pallas_call(
        functools.partial(compact_kernel, experts, capacity, choice),
        out_shape=(
            jax.ShapeDtypeStruct((1, capacity, width), BF16),
            jax.ShapeDtypeStruct((rows, width), BF16),
        ),
        in_specs=[SMEM, VMEM, VMEM] + [ANY] * len(behind),
        out_specs=(VMEM,) * 2,
        compiler_params=params(12),
        name="compact",
    )(at, first, second, *behind)


def expert_kernel(experts, full, extra, k_steps, at_ref, *refs):
    count = len(full) + len(extra)
    rows_in, refs = refs[:count], refs[count:]
    exts, refs = refs[:count], refs[count:]
    gate_own, gate_other, up_own, up_other, down_own, down_other = refs[:6]
    outs, (acc, hidden, weight) = refs[len(refs) - 3 - count : -3], refs[-3:]
    i = pl.program_id(0)
    half = gate_own.shape[2]
    pieces = []
    for j, size in enumerate(full):
        pieces.append((j, None, size))
    for j, (blocks, size) in enumerate(extra):
        for b in range(blocks):
            pieces.append((len(full) + j, b, size))

    def load(source, j, b):
        return source[j][...] if b is None else source[j][b]

    @pl.when(i == 0)
    def _():
        acc[...] = jnp.zeros_like(acc)
        weight[...] = jnp.concatenate(
            [
                jnp.broadcast_to(gate_of(load(exts, j, b), at_ref[0], experts), (size, LANES))
                for j, b, size in pieces
            ],
            axis=0,
        )

    @pl.when(i < k_steps)
    def _():
        x = jnp.concatenate([load(rows_in, j, b).astype(F32) for j, b, _ in pieces], axis=0)
        x = x.astype(BF16)
        for n, ref in enumerate((gate_own, gate_other, up_own, up_other)):
            acc[:, n * half : (n + 1) * half] += jnp.dot(x, ref[0], preferred_element_type=F32)

    @pl.when(i == k_steps - 1)
    def _():
        gate_part = acc[:, : 2 * half]
        hidden[...] = (jax.nn.silu(gate_part) * acc[:, 2 * half :]).astype(BF16)

    @pl.when(i >= k_steps)
    def _():
        own = jnp.dot(hidden[:, :half], down_own[0], preferred_element_type=F32)
        other = jnp.dot(hidden[:, half:], down_other[0], preferred_element_type=F32)
        total = own.astype(BF16).astype(F32) + other.astype(BF16).astype(F32)
        scaled = total.astype(BF16).astype(F32) * weight[:, :1]
        offset = 0
        for j, b, size in pieces:
            part = scaled[offset : offset + size].astype(BF16)
            if b is None:
                outs[j][...] = part
            else:
                outs[j][b] = part
            offset += size


def run_expert(at, full, extra, weights, experts, behind=(), tile=1792):
    own, other = weights
    features, half = own[0].shape[1:]
    k_steps = features // tile
    n_steps = features // tile
    last = features // LANES
    inputs = list(full) + list(extra)
    row_specs, ext_specs, out_specs, out_shape = [], [], [], []
    for array in inputs:
        lead = array.shape[:-1]
        zeros = (0,) * len(lead)
        row_specs.append(
            pl.BlockSpec(lead + (tile,), lambda i, z=zeros: z + (jnp.minimum(i, k_steps - 1),))
        )
        ext_specs.append(pl.BlockSpec(lead + (LANES,), lambda i, z=zeros: z + (last,)))
        out_specs.append(
            pl.BlockSpec(lead + (tile,), lambda i, z=zeros: z + (jnp.maximum(i - k_steps, 0),))
        )
        out_shape.append(jax.ShapeDtypeStruct(lead + (features,), BF16))
    up_spec = pl.BlockSpec((1, tile, half), lambda i: (0, jnp.minimum(i, k_steps - 1), 0))
    down_spec = pl.BlockSpec((1, half, tile), lambda i: (0, 0, jnp.maximum(i - k_steps, 0)))
    total = sum(a.size // a.shape[-1] for a in inputs)
    return pl.pallas_call(
        functools.partial(
            expert_kernel,
            experts,
            tuple(a.shape[0] for a in full),
            tuple(a.shape[:2] for a in extra),
            k_steps,
        ),
        out_shape=tuple(out_shape),
        grid=(k_steps + n_steps,),
        in_specs=[SMEM] + row_specs + ext_specs + [up_spec] * 4 + [down_spec] * 2
        + [ANY] * len(behind),
        out_specs=tuple(out_specs),
        scratch_shapes=[
            pltpu.VMEM((total, 4 * half), F32),
            pltpu.VMEM((total, 2 * half), BF16),
            pltpu.VMEM((total, LANES), F32),
        ],
        compiler_params=params(44, 1),
        cost_estimate=pl.CostEstimate(flops=COST, bytes_accessed=COST, transcendentals=0),
        name="expert",
    )(at, *inputs, *inputs, own[0], other[0], own[1], other[1], own[2], other[2], *behind)


def combine_kernel(experts, capacity, index, adds, at_ref, block_ref, mine_ref, theirs_ref, *refs):
    out_ref = refs[-1]
    features = mine_ref.shape[1]
    onehot = placement(gate_of(block_ref[:, features:], at_ref[1], experts))
    onehot = onehot[:, :capacity].astype(BF16)
    step = 1024
    for start in range(0, features, step):
        columns = slice(start, start + step)
        total = mine_ref[:, columns].astype(F32) + jnp.dot(
            onehot, theirs_ref[index, :, columns], preferred_element_type=F32
        )
        for ref in refs[:adds]:
            total = total + ref[:, columns].astype(F32)
        out_ref[:, columns] = total.astype(BF16)


def combine(at, block, mine, theirs, index, adds, experts, behind=()):
    rows, features = mine.shape
    capacity = theirs.shape[1]
    return pl.pallas_call(
        functools.partial(combine_kernel, experts, capacity, index, len(adds)),
        out_shape=jax.ShapeDtypeStruct((rows, features), BF16),
        in_specs=[SMEM] + [VMEM] * (3 + len(adds)) + [ANY] * len(behind),
        out_specs=VMEM,
        compiler_params=params(14),
        name="combine",
    )(at, block, mine, theirs, *adds, *behind)


def merge_kernel(choice, at_ref, first_ref, second_ref, more_ref, out_ref):
    use_first = at_ref[choice] == 1

    @pl.when(use_first)
    def _():
        out_ref[...] = (first_ref[...].astype(F32) + more_ref[...].astype(F32)).astype(BF16)

    @pl.when(jnp.logical_not(use_first))
    def _():
        out_ref[...] = (second_ref[...].astype(F32) + more_ref[...].astype(F32)).astype(BF16)


def merge(at, choice, first, second, more):
    return pl.pallas_call(
        functools.partial(merge_kernel, choice),
        out_shape=jax.ShapeDtypeStruct(more.shape, BF16),
        in_specs=[SMEM] + [VMEM] * 3,
        out_specs=VMEM,
        compiler_params=params(14),
        name="merge",
    )(at, first, second, more)


DEPTH = 4
FIRST, LOWER, END = 2, 3, 4


def send(array, dz=0, dy=0, dc=0, only=None):
    pairs = []
    for z in range(DEPTH):
        if 0 <= z + dz < DEPTH and (only is None or z in only):
            for y in range(2):
                for c in range(2):
                    pairs.append(((z * 2 + y) * 2 + c, ((z + dz) * 2 + (y ^ dy)) * 2 + (c ^ dc)))
    return lax.ppermute(array, "ep", pairs)


def send_far(array):
    pairs = [(i, i + 12) for i in range(4)] + [(i + 12, i) for i in range(4)]
    return lax.ppermute(array, "ep", pairs)


def after(array, *others):
    return lax.optimization_barrier((array,) + others)[0]


def line_shards(tokens, routes, gates, w_gate, w_up, w_down):
    tok_rows, features = tokens.shape
    topk = routes.shape[1]
    experts = lax.axis_size("ep") // 2
    capacity = 2 * ((tok_rows * topk * 5 + 8 * experts - 1) // (8 * experts))
    chip = lax.axis_index("ep") // 2
    place = chip // 2
    end = (place == 0) | (place == DEPTH - 1)
    at = jnp.stack([chip, chip ^ 1, place == 0, place < DEPTH // 2, end]).astype(jnp.int32)
    block, picked = prepare(at, tokens, routes, gates, experts, capacity)
    other_gate, other_up = send(w_gate, dc=1), send(w_up, dc=1)
    from_left = send(block, dz=1)
    from_right = send(block, dz=-1)
    picked = send(picked[None], dy=1)

    first = (from_left, from_right, picked, other_gate, other_up)
    from_left, from_right, picked, other_gate, other_up = lax.optimization_barrier(first)
    other_down = send(after(w_down, *first), dc=1)
    mid_left = send(from_left, dz=1)
    mid_right = send(from_right, dz=-1)
    near_picked, near = compact(at, FIRST, from_right, from_left, experts, capacity)
    near_picked = send(near_picked, dy=1)

    far = send_far(after(block, mid_left, mid_right, near_picked, other_down))
    mid_picked, mid = compact(at, LOWER, mid_right, mid_left, experts, capacity)
    mid_picked = send(mid_picked, dy=1)
    weights = ((w_gate, w_up, w_down), (other_gate, other_up, other_down))
    block_out, near_out, back, near_back = run_expert(
        at, (block, near), (picked, near_picked), weights, experts
    )

    last_picked, last = compact(
        at, END, far, from_right, experts, capacity, behind=(near_back, mid_picked)
    )
    last_picked = send(last_picked, dy=1)
    mid_out, last_out, mid_back, last_back = run_expert(
        at, (mid, last), (mid_picked, last_picked), weights, experts
    )
    near_back = send(after(near_back, last_picked), dy=1)
    mid_back = send(after(mid_back, near_back), dy=1)
    last_back = send(after(last_back, mid_back), dy=1)
    back = send(after(back, last_back), dy=1)

    near_sum = combine(at, near, near_out, near_back, 0, (), experts)
    mid_sum = combine(at, mid, mid_out, mid_back, 0, (), experts)
    to_right = send(mid_sum, dz=1, only=(0, 1))
    to_left = send(mid_sum, dz=-1, only=(3, 2))
    last_sum = combine(at, last, last_out, last_back, 0, (), experts, behind=(mid_sum,))
    far_home = send_far(last_sum)
    home_left = send(merge(at, FIRST, near_sum, last_sum, to_right), dz=1)
    home_right = send(merge(at, FIRST, near_sum, near_sum, to_left), dz=-1)
    return combine(at, block, block_out, back, 0, (far_home, home_left, home_right), experts)


def partner(shard, axis, stride):
    return lax.ppermute(shard, axis, [(i, i ^ 1 << stride) for i in range(lax.axis_size(axis))])


def plain_to_grid(values):
    magnitude = jnp.abs(values)
    spacing = jnp.full(values.shape, 2.0 ** (-9), jnp.float32)
    for exponent in range(-5, 9):
        spacing = jnp.where(magnitude >= 2.0**exponent, spacing * 2.0, spacing)
    grid_value = jnp.floor(magnitude / spacing + 0.5) * spacing
    return jnp.where(values < 0, -grid_value, grid_value)


def quantize(rows):
    row_count = rows.shape[0]
    feature_count = rows.shape[1]
    blocks = rows.astype(jnp.float32).reshape(row_count, feature_count // 128, 128)
    largest = jnp.max(jnp.abs(blocks), axis=2)
    scales = ((largest + 1e-06) / 448.0).astype(jnp.bfloat16)
    scales = lax.optimization_barrier(scales)
    quantized = plain_to_grid(blocks / scales.astype(jnp.float32)[:, :, None]).astype(jnp.bfloat16)
    return (quantized.reshape(row_count, feature_count), scales)


def half_expert(quantized, scales, weights):
    row_count = quantized.shape[0]
    feature_count = quantized.shape[1]
    blocks = quantized.astype(jnp.float32).reshape(row_count, feature_count // 128, 128)
    restored = (blocks * scales.astype(jnp.float32)[:, :, None]).astype(jnp.bfloat16)
    restored = restored.reshape(row_count, feature_count)
    gate_part = jnp.dot(restored, weights[0], preferred_element_type=jnp.float32)
    up_part = jnp.dot(restored, weights[1], preferred_element_type=jnp.float32)
    hidden = (jax.nn.silu(gate_part) * up_part).astype(jnp.bfloat16)
    return jnp.dot(hidden, weights[2], preferred_element_type=jnp.float32)


def plain_expert(quantized, scales, weights):
    return half_expert(quantized, scales, weights)


def shards(tokens, routes, gates, w_gate, w_up, w_down):
    tok_rows, feature_count = tokens.shape
    topk_count = routes.shape[1]
    slices = lax.axis_size("ep")
    experts = slices // 2
    capacity = 2 * ((tok_rows * topk_count * 5 + 8 * experts - 1) // (8 * experts))
    weights = (w_gate[0], w_up[0], w_down[0])
    quantized, scales = quantize(tokens)
    qblocks = scales.shape[1]
    flat_experts = routes.reshape(-1)
    onehot = (flat_experts[:, None] == jnp.arange(experts, dtype=jnp.int32)[None, :]).astype(
        jnp.int32
    )
    rank = jnp.sum((jnp.cumsum(onehot, axis=0) - onehot) * onehot, axis=1)
    slot_index = flat_experts * capacity + rank
    token_of = jnp.arange(tok_rows * topk_count, dtype=jnp.int32) // topk_count
    table = jnp.full((experts * capacity,), tok_rows, jnp.int32).at[slot_index].set(token_of)
    padded_q = jnp.concatenate([quantized, jnp.zeros((1, feature_count), jnp.bfloat16)], axis=0)
    padded_s = jnp.concatenate([scales, jnp.zeros((1, qblocks), jnp.bfloat16)], axis=0)
    send_q = padded_q[table].reshape(experts, capacity, feature_count)
    send_s = padded_s[table].reshape(experts, capacity, qblocks)
    half_slots = capacity // 2
    split_q = send_q.reshape(slices, half_slots, feature_count)
    split_s = send_s.reshape(slices, half_slots, qblocks)
    mine_q, mine_s = (
        lax.all_to_all(split_q, "ep", split_axis=0, concat_axis=0, tiled=True),
        lax.all_to_all(split_s, "ep", split_axis=0, concat_axis=0, tiled=True),
    )
    other_q, other_s = partner((mine_q, mine_s), "ep", 0)
    leading = lax.axis_index("ep") % 2 == 0
    low_q = jnp.where(leading, mine_q, other_q)
    high_q = jnp.where(leading, other_q, mine_q)
    low_s = jnp.where(leading, mine_s, other_s)
    high_s = jnp.where(leading, other_s, mine_s)
    rows_q = jnp.concatenate([low_q, high_q], axis=1)
    rows_s = jnp.concatenate([low_s, high_s], axis=1)
    senders = rows_q.shape[0]
    partial_value = plain_expert(
        rows_q.reshape(senders * capacity, feature_count),
        rows_s.reshape(senders * capacity, qblocks),
        weights,
    )
    rounded = partial_value.astype(jnp.bfloat16).reshape(senders, capacity, feature_count)
    low_part = rounded[:, :half_slots]
    high_part = rounded[:, half_slots:]
    kept_half = jnp.where(leading, low_part, high_part)
    given_half = jnp.where(leading, high_part, low_part)
    partner_sum = partner(given_half, "ep", 0)
    kept_half = lax.optimization_barrier(kept_half)
    summed = (kept_half.astype(jnp.float32) + partner_sum.astype(jnp.float32)).astype(jnp.bfloat16)
    back = lax.all_to_all(summed, "ep", split_axis=0, concat_axis=0, tiled=True)
    expert_out = back.reshape(experts, capacity, feature_count)
    expert_out = lax.optimization_barrier(expert_out).reshape(experts * capacity, feature_count)
    picked = expert_out[slot_index].reshape(tok_rows, topk_count, feature_count)
    mixed = jnp.einsum("tk,tkd->td", gates, picked.astype(jnp.float32))
    return mixed.astype(jnp.bfloat16)


def solution(mesh):
    placed = (
        P(("groups", "ep"), None),
        P(("groups", "ep"), None),
        P(("groups", "ep"), None),
        P("ep", None, None),
        P("ep", None, None),
        P("ep", None, None),
    )
    line = mesh.shape["ep"] == 4 * DEPTH
    return jax.shard_map(
        line_shards if line else shards, mesh=mesh, in_specs=placed, out_specs=P(("groups", "ep"), None), check_vma=False
    )
```

```python
import functools

import jax
import jax.numpy as jnp
from jax import lax
from jax.experimental import pallas as pl
from jax.experimental.pallas import tpu as pltpu
from jax.sharding import PartitionSpec as P

F32 = jnp.float32
BF16 = jnp.bfloat16
LANES = 128
BLOCK = 128
MIB = 1024 * 1024
COST = 1024


def params(limit, grid_dims=0):
    semantics = ("arbitrary",) * grid_dims if grid_dims else None
    return pltpu.CompilerParams(vmem_limit_bytes=limit * MIB, dimension_semantics=semantics)


SMEM = pl.BlockSpec(memory_space=pltpu.SMEM)
VMEM = pl.BlockSpec(memory_space=pltpu.VMEM)
ANY = pl.BlockSpec(memory_space=pl.ANY)


def to_grid(values):
    scaled = jnp.abs(values) * 512.0
    above = scaled >= 2.0**11
    power = jnp.where(above, 2.0**-1, 2.0**-9)
    scaled = jnp.where(above, scaled * 2.0**-8, scaled)
    for exponent in (4, 2, 1):
        above = scaled >= 2.0 ** (3 + exponent)
        power = jnp.where(above, power * 2.0**exponent, power)
        scaled = jnp.where(above, scaled * 2.0**-exponent, scaled)
    grid_value = jnp.floor(scaled + 0.5) * power
    return jnp.where(values < 0, -grid_value, grid_value)


def gate_of(ext, expert, experts):
    lane = lax.broadcasted_iota(jnp.int32, ext.shape, 1)
    mine = (lane == expert) | (lane == expert + experts) | (lane == expert + 2 * experts)
    return jnp.sum(jnp.where(mine, ext.astype(F32), 0.0), axis=1, keepdims=True)


def placement(gate):
    rows = gate.shape[0]
    routed = gate > 0.0
    before = lax.broadcasted_iota(jnp.int32, (rows, rows), 1) < lax.broadcasted_iota(
        jnp.int32, (rows, rows), 0
    )
    ones = jnp.broadcast_to(jnp.where(routed, 1.0, 0.0), (rows, LANES)).astype(BF16)
    rank = jnp.dot(jnp.where(before, 1.0, 0.0).astype(BF16), ones, preferred_element_type=F32)
    place = lax.broadcasted_iota(jnp.int32, (rows, LANES), 1)
    return jnp.where(routed & (rank.astype(jnp.int32) == place), 1.0, 0.0)


def picker(gate, capacity):
    return placement(gate).T[:capacity].astype(BF16)


def pick_rows(onehot, rows):
    return jnp.dot(onehot, rows, preferred_element_type=F32).astype(BF16)


def prepare_kernel(experts, capacity, at_ref, tokens_ref, routes_ref, gates_ref, x_ref, y_ref):
    rows, features = tokens_ref.shape
    sub = lax.broadcasted_iota(jnp.int32, (LANES, rows), 0)
    value = jnp.zeros((LANES, rows), F32)
    for k in range(routes_ref.shape[0]):
        route = routes_ref[k : k + 1, :]
        hit = (sub == route) | (sub == route + experts) | (sub == route + 2 * experts)
        value = value + jnp.where(hit, gates_ref[k : k + 1, :], 0.0)
    value = value.T
    lane = lax.broadcasted_iota(jnp.int32, (rows, LANES), 1)
    high = value.astype(BF16).astype(F32)
    middle = (value - high).astype(BF16).astype(F32)
    low = value - high - middle
    ext = jnp.where(lane < experts, high, jnp.where(lane < 2 * experts, middle, low)).astype(BF16)
    onehot = picker(gate_of(ext, at_ref[1], experts), capacity)
    x_ref[:, features:] = ext
    y_ref[:, features:] = pick_rows(onehot, ext)
    step = 4 * BLOCK

    def body(i, carry):
        start = pl.multiple_of(i * step, step)
        tokens = tokens_ref[:, pl.ds(start, step)].astype(F32)
        parts = []
        for b in range(step // BLOCK):
            block = tokens[:, b * BLOCK : (b + 1) * BLOCK]
            largest = jnp.max(jnp.abs(block), axis=1, keepdims=True)
            scale = ((largest + 1e-06) / 448.0).astype(BF16).astype(F32)
            parts.append((to_grid(block / scale) * scale).astype(BF16))
        restored = jnp.concatenate(parts, axis=1)
        x_ref[:, pl.ds(start, step)] = restored
        y_ref[:, pl.ds(start, step)] = pick_rows(onehot, restored)
        return carry

    lax.fori_loop(0, features // step, body, 0, unroll=2)


def prepare(at, tokens, routes, gates, experts, capacity):
    rows, features = tokens.shape
    width = features + LANES
    return pl.pallas_call(
        functools.partial(prepare_kernel, experts, capacity),
        out_shape=(
            jax.ShapeDtypeStruct((rows, width), BF16),
            jax.ShapeDtypeStruct((capacity, width), BF16),
        ),
        in_specs=[SMEM] + [VMEM] * 3,
        out_specs=(VMEM,) * 2,
        compiler_params=params(12),
        name="prepare",
    )(at, tokens, routes.T, gates.T)


def compact_kernel(experts, capacity, choice, at_ref, first_ref, second_ref, *refs):
    picked_ref, block_ref = refs[-2:]
    features = first_ref.shape[1] - LANES
    use_first = at_ref[choice] == 1

    @pl.when(use_first)
    def _():
        block_ref[...] = first_ref[...]

    @pl.when(jnp.logical_not(use_first))
    def _():
        block_ref[...] = second_ref[...]

    ext = block_ref[:, features:]
    onehot = picker(gate_of(ext, at_ref[1], experts), capacity)
    picked_ref[0, :, features:] = pick_rows(onehot, ext)
    step = 1024
    for start in range(0, features, step):
        columns = slice(start, start + step)
        picked_ref[0, :, columns] = pick_rows(onehot, block_ref[:, columns])


def compact(at, choice, first, second, experts, capacity, behind=()):
    rows, width = first.shape
    return pl.pallas_call(
        functools.partial(compact_kernel, experts, capacity, choice),
        out_shape=(
            jax.ShapeDtypeStruct((1, capacity, width), BF16),
            jax.ShapeDtypeStruct((rows, width), BF16),
        ),
        in_specs=[SMEM, VMEM, VMEM] + [ANY] * len(behind),
        out_specs=(VMEM,) * 2,
        compiler_params=params(12),
        name="compact",
    )(at, first, second, *behind)


def expert_kernel(experts, full, extra, k_steps, at_ref, *refs):
    count = len(full) + len(extra)
    rows_in, refs = refs[:count], refs[count:]
    exts, refs = refs[:count], refs[count:]
    gate_own, gate_other, up_own, up_other, down_own, down_other = refs[:6]
    outs, (acc, hidden, weight) = refs[len(refs) - 3 - count : -3], refs[-3:]
    i = pl.program_id(0)
    half = gate_own.shape[2]
    pieces = []
    for j, size in enumerate(full):
        pieces.append((j, None, size))
    for j, (blocks, size) in enumerate(extra):
        for b in range(blocks):
            pieces.append((len(full) + j, b, size))

    def load(source, j, b):
        return source[j][...] if b is None else source[j][b]

    @pl.when(i == 0)
    def _():
        acc[...] = jnp.zeros_like(acc)
        weight[...] = jnp.concatenate(
            [
                jnp.broadcast_to(gate_of(load(exts, j, b), at_ref[0], experts), (size, LANES))
                for j, b, size in pieces
            ],
            axis=0,
        )

    @pl.when(i < k_steps)
    def _():
        x = jnp.concatenate([load(rows_in, j, b).astype(F32) for j, b, _ in pieces], axis=0)
        x = x.astype(BF16)
        for n, ref in enumerate((gate_own, gate_other, up_own, up_other)):
            acc[:, n * half : (n + 1) * half] += jnp.dot(x, ref[0], preferred_element_type=F32)

    @pl.when(i == k_steps - 1)
    def _():
        gate_part = acc[:, : 2 * half]
        hidden[...] = (jax.nn.silu(gate_part) * acc[:, 2 * half :]).astype(BF16)

    @pl.when(i >= k_steps)
    def _():
        own = jnp.dot(hidden[:, :half], down_own[0], preferred_element_type=F32)
        other = jnp.dot(hidden[:, half:], down_other[0], preferred_element_type=F32)
        total = own.astype(BF16).astype(F32) + other.astype(BF16).astype(F32)
        scaled = total.astype(BF16).astype(F32) * weight[:, :1]
        offset = 0
        for j, b, size in pieces:
            part = scaled[offset : offset + size].astype(BF16)
            if b is None:
                outs[j][...] = part
            else:
                outs[j][b] = part
            offset += size


def run_expert(at, full, extra, weights, experts, behind=(), tile=1792):
    own, other = weights
    features, half = own[0].shape[1:]
    k_steps = features // tile
    n_steps = features // tile
    last = features // LANES
    inputs = list(full) + list(extra)
    row_specs, ext_specs, out_specs, out_shape = [], [], [], []
    for array in inputs:
        lead = array.shape[:-1]
        zeros = (0,) * len(lead)
        row_specs.append(
            pl.BlockSpec(lead + (tile,), lambda i, z=zeros: z + (jnp.minimum(i, k_steps - 1),))
        )
        ext_specs.append(pl.BlockSpec(lead + (LANES,), lambda i, z=zeros: z + (last,)))
        out_specs.append(
            pl.BlockSpec(lead + (tile,), lambda i, z=zeros: z + (jnp.maximum(i - k_steps, 0),))
        )
        out_shape.append(jax.ShapeDtypeStruct(lead + (features,), BF16))
    up_spec = pl.BlockSpec((1, tile, half), lambda i: (0, jnp.minimum(i, k_steps - 1), 0))
    down_spec = pl.BlockSpec((1, half, tile), lambda i: (0, 0, jnp.maximum(i - k_steps, 0)))
    total = sum(a.size // a.shape[-1] for a in inputs)
    return pl.pallas_call(
        functools.partial(
            expert_kernel,
            experts,
            tuple(a.shape[0] for a in full),
            tuple(a.shape[:2] for a in extra),
            k_steps,
        ),
        out_shape=tuple(out_shape),
        grid=(k_steps + n_steps,),
        in_specs=[SMEM] + row_specs + ext_specs + [up_spec] * 4 + [down_spec] * 2
        + [ANY] * len(behind),
        out_specs=tuple(out_specs),
        scratch_shapes=[
            pltpu.VMEM((total, 4 * half), F32),
            pltpu.VMEM((total, 2 * half), BF16),
            pltpu.VMEM((total, LANES), F32),
        ],
        compiler_params=params(34, 1),
        cost_estimate=pl.CostEstimate(flops=COST, bytes_accessed=COST, transcendentals=0),
        name="expert",
    )(at, *inputs, *inputs, own[0], other[0], own[1], other[1], own[2], other[2], *behind)


def combine_kernel(experts, capacity, index, adds, at_ref, block_ref, mine_ref, theirs_ref, *refs):
    out_ref = refs[-1]
    features = mine_ref.shape[1]
    onehot = placement(gate_of(block_ref[:, features:], at_ref[1], experts))
    onehot = onehot[:, :capacity].astype(BF16)
    step = 1024
    for start in range(0, features, step):
        columns = slice(start, start + step)
        total = mine_ref[:, columns].astype(F32) + jnp.dot(
            onehot, theirs_ref[index, :, columns], preferred_element_type=F32
        )
        for ref in refs[:adds]:
            total = total + ref[:, columns].astype(F32)
        out_ref[:, columns] = total.astype(BF16)


def combine(at, block, mine, theirs, index, adds, experts, behind=()):
    rows, features = mine.shape
    capacity = theirs.shape[1]
    return pl.pallas_call(
        functools.partial(combine_kernel, experts, capacity, index, len(adds)),
        out_shape=jax.ShapeDtypeStruct((rows, features), BF16),
        in_specs=[SMEM] + [VMEM] * (3 + len(adds)) + [ANY] * len(behind),
        out_specs=VMEM,
        compiler_params=params(14),
        name="combine",
    )(at, block, mine, theirs, *adds, *behind)


def merge_kernel(choice, at_ref, first_ref, second_ref, more_ref, out_ref):
    use_first = at_ref[choice] == 1

    @pl.when(use_first)
    def _():
        out_ref[...] = (first_ref[...].astype(F32) + more_ref[...].astype(F32)).astype(BF16)

    @pl.when(jnp.logical_not(use_first))
    def _():
        out_ref[...] = (second_ref[...].astype(F32) + more_ref[...].astype(F32)).astype(BF16)


def merge(at, choice, first, second, more):
    return pl.pallas_call(
        functools.partial(merge_kernel, choice),
        out_shape=jax.ShapeDtypeStruct(more.shape, BF16),
        in_specs=[SMEM] + [VMEM] * 3,
        out_specs=VMEM,
        compiler_params=params(14),
        name="merge",
    )(at, first, second, more)


DEPTH = 4
FIRST, LOWER, END = 2, 3, 4


def send(array, dz=0, dy=0, dc=0, only=None):
    pairs = []
    for z in range(DEPTH):
        if 0 <= z + dz < DEPTH and (only is None or z in only):
            for y in range(2):
                for c in range(2):
                    pairs.append(((z * 2 + y) * 2 + c, ((z + dz) * 2 + (y ^ dy)) * 2 + (c ^ dc)))
    return lax.ppermute(array, "ep", pairs)


def send_far(array):
    pairs = [(i, i + 12) for i in range(4)] + [(i + 12, i) for i in range(4)]
    return lax.ppermute(array, "ep", pairs)


def after(array, *others):
    return lax.optimization_barrier((array,) + others)[0]


def line_shards(tokens, routes, gates, w_gate, w_up, w_down):
    tok_rows, features = tokens.shape
    topk = routes.shape[1]
    experts = lax.axis_size("ep") // 2
    capacity = 2 * ((tok_rows * topk * 5 + 8 * experts - 1) // (8 * experts))
    chip = lax.axis_index("ep") // 2
    place = chip // 2
    end = (place == 0) | (place == DEPTH - 1)
    at = jnp.stack([chip, chip ^ 1, place == 0, place < DEPTH // 2, end]).astype(jnp.int32)
    block, picked = prepare(at, tokens, routes, gates, experts, capacity)
    other = tuple(send(w, dc=1) for w in (w_gate, w_up, w_down))
    from_left = send(block, dz=1)
    from_right = send(block, dz=-1)

    first = (from_left, from_right, picked) + other
    from_left, from_right, picked, *other = lax.optimization_barrier(first)
    weights = ((w_gate, w_up, w_down), other)
    mid_left = send(from_left, dz=1)
    mid_right = send(from_right, dz=-1)
    near_picked, near = compact(at, FIRST, from_right, from_left, experts, capacity)
    near_picked = send(near_picked, dy=1)
    picked = send(picked[None], dy=1)
    block_out, near_out = run_expert(at, (block, near), (), weights, experts)

    far = send_far(after(block, mid_left, mid_right, block_out, near_picked))
    mid_picked, mid = compact(
        at, LOWER, mid_right, mid_left, experts, capacity, behind=(picked,)
    )
    mid_picked = send(mid_picked, dy=1)
    mid_out, back, near_back = run_expert(at, (mid,), (picked, near_picked), weights, experts)

    last_picked, last = compact(
        at, END, far, from_right, experts, capacity, behind=(near_back, mid_picked)
    )
    last_picked = send(last_picked, dy=1)
    last_out, mid_back, last_back = run_expert(
        at, (last,), (mid_picked, last_picked), weights, experts
    )
    near_back = send(after(near_back, last_picked), dy=1)
    mid_back = send(after(mid_back, near_back), dy=1)
    last_back = send(after(last_back, mid_back), dy=1)
    back = send(after(back, last_back), dy=1)

    near_sum = combine(at, near, near_out, near_back, 0, (), experts)
    mid_sum = combine(at, mid, mid_out, mid_back, 0, (), experts)
    to_right = send(mid_sum, dz=1, only=(0, 1))
    to_left = send(mid_sum, dz=-1, only=(3, 2))
    last_sum = combine(at, last, last_out, last_back, 0, (), experts, behind=(mid_sum,))
    far_home = send_far(last_sum)
    home_left = send(merge(at, FIRST, near_sum, last_sum, to_right), dz=1)
    home_right = send(merge(at, FIRST, near_sum, near_sum, to_left), dz=-1)
    return combine(at, block, block_out, back, 0, (far_home, home_left, home_right), experts)


def partner(shard, axis, stride):
    return lax.ppermute(shard, axis, [(i, i ^ 1 << stride) for i in range(lax.axis_size(axis))])


def plain_to_grid(values):
    magnitude = jnp.abs(values)
    spacing = jnp.full(values.shape, 2.0 ** (-9), jnp.float32)
    for exponent in range(-5, 9):
        spacing = jnp.where(magnitude >= 2.0**exponent, spacing * 2.0, spacing)
    grid_value = jnp.floor(magnitude / spacing + 0.5) * spacing
    return jnp.where(values < 0, -grid_value, grid_value)


def quantize(rows):
    row_count = rows.shape[0]
    feature_count = rows.shape[1]
    blocks = rows.astype(jnp.float32).reshape(row_count, feature_count // 128, 128)
    largest = jnp.max(jnp.abs(blocks), axis=2)
    scales = ((largest + 1e-06) / 448.0).astype(jnp.bfloat16)
    scales = lax.optimization_barrier(scales)
    quantized = plain_to_grid(blocks / scales.astype(jnp.float32)[:, :, None]).astype(jnp.bfloat16)
    return (quantized.reshape(row_count, feature_count), scales)


def half_expert(quantized, scales, weights):
    row_count = quantized.shape[0]
    feature_count = quantized.shape[1]
    blocks = quantized.astype(jnp.float32).reshape(row_count, feature_count // 128, 128)
    restored = (blocks * scales.astype(jnp.float32)[:, :, None]).astype(jnp.bfloat16)
    restored = restored.reshape(row_count, feature_count)
    gate_part = jnp.dot(restored, weights[0], preferred_element_type=jnp.float32)
    up_part = jnp.dot(restored, weights[1], preferred_element_type=jnp.float32)
    hidden = (jax.nn.silu(gate_part) * up_part).astype(jnp.bfloat16)
    return jnp.dot(hidden, weights[2], preferred_element_type=jnp.float32)


def plain_expert(quantized, scales, weights):
    return half_expert(quantized, scales, weights)


def shards(tokens, routes, gates, w_gate, w_up, w_down):
    tok_rows, feature_count = tokens.shape
    topk_count = routes.shape[1]
    slices = lax.axis_size("ep")
    experts = slices // 2
    capacity = 2 * ((tok_rows * topk_count * 5 + 8 * experts - 1) // (8 * experts))
    weights = (w_gate[0], w_up[0], w_down[0])
    quantized, scales = quantize(tokens)
    qblocks = scales.shape[1]
    flat_experts = routes.reshape(-1)
    onehot = (flat_experts[:, None] == jnp.arange(experts, dtype=jnp.int32)[None, :]).astype(
        jnp.int32
    )
    rank = jnp.sum((jnp.cumsum(onehot, axis=0) - onehot) * onehot, axis=1)
    slot_index = flat_experts * capacity + rank
    token_of = jnp.arange(tok_rows * topk_count, dtype=jnp.int32) // topk_count
    table = jnp.full((experts * capacity,), tok_rows, jnp.int32).at[slot_index].set(token_of)
    padded_q = jnp.concatenate([quantized, jnp.zeros((1, feature_count), jnp.bfloat16)], axis=0)
    padded_s = jnp.concatenate([scales, jnp.zeros((1, qblocks), jnp.bfloat16)], axis=0)
    send_q = padded_q[table].reshape(experts, capacity, feature_count)
    send_s = padded_s[table].reshape(experts, capacity, qblocks)
    half_slots = capacity // 2
    split_q = send_q.reshape(slices, half_slots, feature_count)
    split_s = send_s.reshape(slices, half_slots, qblocks)
    mine_q, mine_s = (
        lax.all_to_all(split_q, "ep", split_axis=0, concat_axis=0, tiled=True),
        lax.all_to_all(split_s, "ep", split_axis=0, concat_axis=0, tiled=True),
    )
    other_q, other_s = partner((mine_q, mine_s), "ep", 0)
    leading = lax.axis_index("ep") % 2 == 0
    low_q = jnp.where(leading, mine_q, other_q)
    high_q = jnp.where(leading, other_q, mine_q)
    low_s = jnp.where(leading, mine_s, other_s)
    high_s = jnp.where(leading, other_s, mine_s)
    rows_q = jnp.concatenate([low_q, high_q], axis=1)
    rows_s = jnp.concatenate([low_s, high_s], axis=1)
    senders = rows_q.shape[0]
    partial_value = plain_expert(
        rows_q.reshape(senders * capacity, feature_count),
        rows_s.reshape(senders * capacity, qblocks),
        weights,
    )
    rounded = partial_value.astype(jnp.bfloat16).reshape(senders, capacity, feature_count)
    low_part = rounded[:, :half_slots]
    high_part = rounded[:, half_slots:]
    kept_half = jnp.where(leading, low_part, high_part)
    given_half = jnp.where(leading, high_part, low_part)
    partner_sum = partner(given_half, "ep", 0)
    kept_half = lax.optimization_barrier(kept_half)
    summed = (kept_half.astype(jnp.float32) + partner_sum.astype(jnp.float32)).astype(jnp.bfloat16)
    back = lax.all_to_all(summed, "ep", split_axis=0, concat_axis=0, tiled=True)
    expert_out = back.reshape(experts, capacity, feature_count)
    expert_out = lax.optimization_barrier(expert_out).reshape(experts * capacity, feature_count)
    picked = expert_out[slot_index].reshape(tok_rows, topk_count, feature_count)
    mixed = jnp.einsum("tk,tkd->td", gates, picked.astype(jnp.float32))
    return mixed.astype(jnp.bfloat16)


def solution(mesh):
    placed = (
        P(("groups", "ep"), None),
        P(("groups", "ep"), None),
        P(("groups", "ep"), None),
        P("ep", None, None),
        P("ep", None, None),
        P("ep", None, None),
    )
    line = mesh.shape["ep"] == 4 * DEPTH
    return jax.shard_map(
        line_shards if line else shards, mesh=mesh, in_specs=placed, out_specs=P(("groups", "ep"), None), check_vma=False
    )
```

```python
import functools

import jax
import jax.numpy as jnp
from jax import lax
from jax.experimental import pallas as pl
from jax.experimental.pallas import tpu as pltpu
from jax.sharding import PartitionSpec as P

F32 = jnp.float32
BF16 = jnp.bfloat16
LANES = 128
BLOCK = 128
MIB = 1024 * 1024
COST = 1024


def params(limit, grid_dims=0):
    semantics = ("arbitrary",) * grid_dims if grid_dims else None
    return pltpu.CompilerParams(vmem_limit_bytes=limit * MIB, dimension_semantics=semantics)


SMEM = pl.BlockSpec(memory_space=pltpu.SMEM)
VMEM = pl.BlockSpec(memory_space=pltpu.VMEM)
ANY = pl.BlockSpec(memory_space=pl.ANY)


def to_grid(values):
    scaled = jnp.abs(values) * 512.0
    above = scaled >= 2.0**11
    power = jnp.where(above, 2.0**-1, 2.0**-9)
    scaled = jnp.where(above, scaled * 2.0**-8, scaled)
    for exponent in (4, 2, 1):
        above = scaled >= 2.0 ** (3 + exponent)
        power = jnp.where(above, power * 2.0**exponent, power)
        scaled = jnp.where(above, scaled * 2.0**-exponent, scaled)
    grid_value = jnp.floor(scaled + 0.5) * power
    return jnp.where(values < 0, -grid_value, grid_value)


def gate_of(ext, expert, experts):
    lane = lax.broadcasted_iota(jnp.int32, ext.shape, 1)
    mine = (lane == expert) | (lane == expert + experts) | (lane == expert + 2 * experts)
    return jnp.sum(jnp.where(mine, ext.astype(F32), 0.0), axis=1, keepdims=True)


def placement(gate):
    rows = gate.shape[0]
    routed = gate > 0.0
    before = lax.broadcasted_iota(jnp.int32, (rows, rows), 1) < lax.broadcasted_iota(
        jnp.int32, (rows, rows), 0
    )
    ones = jnp.broadcast_to(jnp.where(routed, 1.0, 0.0), (rows, LANES)).astype(BF16)
    rank = jnp.dot(jnp.where(before, 1.0, 0.0).astype(BF16), ones, preferred_element_type=F32)
    place = lax.broadcasted_iota(jnp.int32, (rows, LANES), 1)
    return jnp.where(routed & (rank.astype(jnp.int32) == place), 1.0, 0.0)


def picker(gate, capacity):
    return placement(gate).T[:capacity].astype(BF16)


def pick_rows(onehot, rows):
    return jnp.dot(onehot, rows, preferred_element_type=F32).astype(BF16)


def prepare_kernel(experts, tokens_ref, routes_ref, gates_ref, x_ref):
    rows, features = tokens_ref.shape
    sub = lax.broadcasted_iota(jnp.int32, (LANES, rows), 0)
    value = jnp.zeros((LANES, rows), F32)
    for k in range(routes_ref.shape[0]):
        route = routes_ref[k : k + 1, :]
        hit = (sub == route) | (sub == route + experts) | (sub == route + 2 * experts)
        value = value + jnp.where(hit, gates_ref[k : k + 1, :], 0.0)
    value = value.T
    lane = lax.broadcasted_iota(jnp.int32, (rows, LANES), 1)
    high = value.astype(BF16).astype(F32)
    middle = (value - high).astype(BF16).astype(F32)
    low = value - high - middle
    ext = jnp.where(lane < experts, high, jnp.where(lane < 2 * experts, middle, low)).astype(BF16)
    x_ref[:, features:] = ext
    step = 4 * BLOCK

    def body(i, carry):
        start = pl.multiple_of(i * step, step)
        tokens = tokens_ref[:, pl.ds(start, step)].astype(F32)
        parts = []
        for b in range(step // BLOCK):
            block = tokens[:, b * BLOCK : (b + 1) * BLOCK]
            largest = jnp.max(jnp.abs(block), axis=1, keepdims=True)
            scale = ((largest + 1e-06) / 448.0).astype(BF16).astype(F32)
            parts.append((to_grid(block / scale) * scale).astype(BF16))
        x_ref[:, pl.ds(start, step)] = jnp.concatenate(parts, axis=1)
        return carry

    lax.fori_loop(0, features // step, body, 0, unroll=2)


def prepare(tokens, routes, gates, experts):
    rows, features = tokens.shape
    return pl.pallas_call(
        functools.partial(prepare_kernel, experts),
        out_shape=jax.ShapeDtypeStruct((rows, features + LANES), BF16),
        in_specs=[VMEM] * 3,
        out_specs=VMEM,
        compiler_params=params(12),
        name="prepare",
    )(tokens, routes.T, gates.T)


def compact_kernel(experts, capacity, choice, at_ref, first_ref, second_ref, *refs):
    picked_ref, block_ref = refs[-2:]
    features = first_ref.shape[1] - LANES
    use_first = at_ref[choice] == 1

    @pl.when(use_first)
    def _():
        block_ref[...] = first_ref[...]

    @pl.when(jnp.logical_not(use_first))
    def _():
        block_ref[...] = second_ref[...]

    ext = block_ref[:, features:]
    onehot = picker(gate_of(ext, at_ref[1], experts), capacity)
    picked_ref[0, :, features:] = pick_rows(onehot, ext)
    step = 1024
    for start in range(0, features, step):
        columns = slice(start, start + step)
        picked_ref[0, :, columns] = pick_rows(onehot, block_ref[:, columns])


def compact(at, choice, first, second, experts, capacity, behind=()):
    rows, width = first.shape
    return pl.pallas_call(
        functools.partial(compact_kernel, experts, capacity, choice),
        out_shape=(
            jax.ShapeDtypeStruct((1, capacity, width), BF16),
            jax.ShapeDtypeStruct((rows, width), BF16),
        ),
        in_specs=[SMEM, VMEM, VMEM] + [ANY] * len(behind),
        out_specs=(VMEM,) * 2,
        compiler_params=params(12),
        name="compact",
    )(at, first, second, *behind)


def expert_kernel(experts, full, extra, k_steps, at_ref, *refs):
    count = len(full) + len(extra)
    rows_in, refs = refs[:count], refs[count:]
    exts, refs = refs[:count], refs[count:]
    gate_own, gate_other, up_own, up_other, down_own, down_other = refs[:6]
    outs, (acc, hidden, weight) = refs[len(refs) - 3 - count : -3], refs[-3:]
    i = pl.program_id(0)
    half = gate_own.shape[2]
    pieces = []
    for j, size in enumerate(full):
        pieces.append((j, None, size))
    for j, (blocks, size) in enumerate(extra):
        for b in range(blocks):
            pieces.append((len(full) + j, b, size))

    def load(source, j, b):
        return source[j][...] if b is None else source[j][b]

    @pl.when(i == 0)
    def _():
        acc[...] = jnp.zeros_like(acc)
        weight[...] = jnp.concatenate(
            [
                jnp.broadcast_to(gate_of(load(exts, j, b), at_ref[0], experts), (size, LANES))
                for j, b, size in pieces
            ],
            axis=0,
        )

    @pl.when(i < k_steps)
    def _():
        x = jnp.concatenate([load(rows_in, j, b).astype(F32) for j, b, _ in pieces], axis=0)
        x = x.astype(BF16)
        for n, ref in enumerate((gate_own, gate_other, up_own, up_other)):
            acc[:, n * half : (n + 1) * half] += jnp.dot(x, ref[0], preferred_element_type=F32)

    @pl.when(i == k_steps - 1)
    def _():
        gate_part = acc[:, : 2 * half]
        hidden[...] = (jax.nn.silu(gate_part) * acc[:, 2 * half :]).astype(BF16)

    @pl.when(i >= k_steps)
    def _():
        own = jnp.dot(hidden[:, :half], down_own[0], preferred_element_type=F32)
        other = jnp.dot(hidden[:, half:], down_other[0], preferred_element_type=F32)
        total = own.astype(BF16).astype(F32) + other.astype(BF16).astype(F32)
        scaled = total.astype(BF16).astype(F32) * weight[:, :1]
        offset = 0
        for j, b, size in pieces:
            part = scaled[offset : offset + size].astype(BF16)
            if b is None:
                outs[j][...] = part
            else:
                outs[j][b] = part
            offset += size


def run_expert(at, full, extra, weights, experts, behind=(), tile=1792):
    own, other = weights
    features, half = own[0].shape[1:]
    k_steps = features // tile
    n_steps = features // tile
    last = features // LANES
    inputs = list(full) + list(extra)
    row_specs, ext_specs, out_specs, out_shape = [], [], [], []
    for array in inputs:
        lead = array.shape[:-1]
        zeros = (0,) * len(lead)
        row_specs.append(
            pl.BlockSpec(lead + (tile,), lambda i, z=zeros: z + (jnp.minimum(i, k_steps - 1),))
        )
        ext_specs.append(pl.BlockSpec(lead + (LANES,), lambda i, z=zeros: z + (last,)))
        out_specs.append(
            pl.BlockSpec(lead + (tile,), lambda i, z=zeros: z + (jnp.maximum(i - k_steps, 0),))
        )
        out_shape.append(jax.ShapeDtypeStruct(lead + (features,), BF16))
    up_spec = pl.BlockSpec((1, tile, half), lambda i: (0, jnp.minimum(i, k_steps - 1), 0))
    down_spec = pl.BlockSpec((1, half, tile), lambda i: (0, 0, jnp.maximum(i - k_steps, 0)))
    total = sum(a.size // a.shape[-1] for a in inputs)
    return pl.pallas_call(
        functools.partial(
            expert_kernel,
            experts,
            tuple(a.shape[0] for a in full),
            tuple(a.shape[:2] for a in extra),
            k_steps,
        ),
        out_shape=tuple(out_shape),
        grid=(k_steps + n_steps,),
        in_specs=[SMEM] + row_specs + ext_specs + [up_spec] * 4 + [down_spec] * 2
        + [ANY] * len(behind),
        out_specs=tuple(out_specs),
        scratch_shapes=[
            pltpu.VMEM((total, 4 * half), F32),
            pltpu.VMEM((total, 2 * half), BF16),
            pltpu.VMEM((total, LANES), F32),
        ],
        compiler_params=params(46, 1),
        cost_estimate=pl.CostEstimate(flops=COST, bytes_accessed=COST, transcendentals=0),
        name="expert",
    )(at, *inputs, *inputs, own[0], other[0], own[1], other[1], own[2], other[2], *behind)


def expert_up_kernel(experts, k_steps, at_ref, whole_ref, some_ref, *refs):
    whole_ext, some_ext, gate_own, gate_other, up_own, up_other = refs[:6]
    hidden_ref, weight_ref, acc = refs[-3:]
    i = pl.program_id(0)
    half = gate_own.shape[2]

    @pl.when(i == 0)
    def _():
        acc[...] = jnp.zeros_like(acc)
        gates = [gate_of(ext, at_ref[0], experts) for ext in (whole_ext[...], some_ext[0])]
        weight_ref[...] = jnp.broadcast_to(jnp.concatenate(gates, axis=0), weight_ref.shape)

    x = jnp.concatenate([whole_ref[...].astype(F32), some_ref[0].astype(F32)], axis=0)
    x = x.astype(BF16)
    for n, ref in enumerate((gate_own, gate_other, up_own, up_other)):
        acc[:, n * half : (n + 1) * half] += jnp.dot(x, ref[0], preferred_element_type=F32)

    @pl.when(i == k_steps - 1)
    def _():
        hidden_ref[...] = (jax.nn.silu(acc[:, : 2 * half]) * acc[:, 2 * half :]).astype(BF16)


def expert_up(at, whole, some, weights, experts, tile=1792):
    own, other = weights
    features, half = own[0].shape[1:]
    rows, capacity = whole.shape[0], some.shape[1]
    total = rows + capacity
    last = features // LANES
    up_spec = pl.BlockSpec((1, tile, half), lambda i: (0, i, 0))
    return pl.pallas_call(
        functools.partial(expert_up_kernel, experts, features // tile),
        out_shape=(
            jax.ShapeDtypeStruct((total, 2 * half), BF16),
            jax.ShapeDtypeStruct((total, LANES), F32),
        ),
        grid=(features // tile,),
        in_specs=[
            SMEM,
            pl.BlockSpec((rows, tile), lambda i: (0, i)),
            pl.BlockSpec((1, capacity, tile), lambda i: (0, 0, i)),
            pl.BlockSpec((rows, LANES), lambda i: (0, last)),
            pl.BlockSpec((1, capacity, LANES), lambda i: (0, 0, last)),
        ]
        + [up_spec] * 4,
        out_specs=(
            pl.BlockSpec((total, 2 * half), lambda i: (0, 0)),
            pl.BlockSpec((total, LANES), lambda i: (0, 0)),
        ),
        scratch_shapes=[pltpu.VMEM((total, 4 * half), F32)],
        compiler_params=params(46, 1),
        cost_estimate=pl.CostEstimate(flops=COST, bytes_accessed=COST, transcendentals=0),
        name="expert_up",
    )(at, whole, some, whole, some, own[0], other[0], own[1], other[1])


def expert_down_kernel(hidden_ref, weight_ref, down_own, down_other, *refs):
    whole_out, some_out = refs[-2:]
    half = down_own.shape[1]
    rows = whole_out.shape[0]
    own = jnp.dot(hidden_ref[:, :half], down_own[0], preferred_element_type=F32)
    other = jnp.dot(hidden_ref[:, half:], down_other[0], preferred_element_type=F32)
    total = own.astype(BF16).astype(F32) + other.astype(BF16).astype(F32)
    scaled = total.astype(BF16).astype(F32) * weight_ref[:, :1]
    whole_out[...] = scaled[:rows].astype(BF16)
    some_out[0] = scaled[rows:].astype(BF16)


def expert_down(hidden, weight, rows, weights, behind=(), tile=1792):
    own, other = weights
    half, features = own[2].shape[1:]
    capacity = hidden.shape[0] - rows
    down_spec = pl.BlockSpec((1, half, tile), lambda i: (0, 0, i))
    return pl.pallas_call(
        expert_down_kernel,
        out_shape=(
            jax.ShapeDtypeStruct((rows, features), BF16),
            jax.ShapeDtypeStruct((1, capacity, features), BF16),
        ),
        grid=(features // tile,),
        in_specs=[pl.BlockSpec(a.shape, lambda i: (0, 0)) for a in (hidden, weight)]
        + [down_spec] * 2
        + [ANY] * len(behind),
        out_specs=(
            pl.BlockSpec((rows, tile), lambda i: (0, i)),
            pl.BlockSpec((1, capacity, tile), lambda i: (0, 0, i)),
        ),
        compiler_params=params(46, 1),
        cost_estimate=pl.CostEstimate(flops=COST, bytes_accessed=COST, transcendentals=0),
        name="expert_down",
    )(hidden, weight, own[2], other[2], *behind)


def combine_kernel(experts, capacity, index, adds, at_ref, block_ref, mine_ref, theirs_ref, *refs):
    out_ref = refs[-1]
    features = mine_ref.shape[1]
    onehot = placement(gate_of(block_ref[:, features:], at_ref[1], experts))
    onehot = onehot[:, :capacity].astype(BF16)
    step = 1024
    for start in range(0, features, step):
        columns = slice(start, start + step)
        total = mine_ref[:, columns].astype(F32) + jnp.dot(
            onehot, theirs_ref[index, :, columns], preferred_element_type=F32
        )
        for ref in refs[:adds]:
            total = total + ref[:, columns].astype(F32)
        out_ref[:, columns] = total.astype(BF16)


def combine(at, block, mine, theirs, index, adds, experts, behind=()):
    rows, features = mine.shape
    capacity = theirs.shape[1]
    return pl.pallas_call(
        functools.partial(combine_kernel, experts, capacity, index, len(adds)),
        out_shape=jax.ShapeDtypeStruct((rows, features), BF16),
        in_specs=[SMEM] + [VMEM] * (3 + len(adds)) + [ANY] * len(behind),
        out_specs=VMEM,
        compiler_params=params(14),
        name="combine",
    )(at, block, mine, theirs, *adds, *behind)


def merge_kernel(choice, at_ref, first_ref, second_ref, more_ref, out_ref):
    use_first = at_ref[choice] == 1

    @pl.when(use_first)
    def _():
        out_ref[...] = (first_ref[...].astype(F32) + more_ref[...].astype(F32)).astype(BF16)

    @pl.when(jnp.logical_not(use_first))
    def _():
        out_ref[...] = (second_ref[...].astype(F32) + more_ref[...].astype(F32)).astype(BF16)


def merge(at, choice, first, second, more):
    return pl.pallas_call(
        functools.partial(merge_kernel, choice),
        out_shape=jax.ShapeDtypeStruct(more.shape, BF16),
        in_specs=[SMEM] + [VMEM] * 3,
        out_specs=VMEM,
        compiler_params=params(14),
        name="merge",
    )(at, first, second, more)


DEPTH = 4
FIRST, LOWER, END = 2, 3, 4


def send(array, dz=0, dy=0, dc=0, only=None):
    pairs = []
    for z in range(DEPTH):
        if 0 <= z + dz < DEPTH and (only is None or z in only):
            for y in range(2):
                for c in range(2):
                    pairs.append(((z * 2 + y) * 2 + c, ((z + dz) * 2 + (y ^ dy)) * 2 + (c ^ dc)))
    return lax.ppermute(array, "ep", pairs)


def send_far(array):
    pairs = [(i, i + 12) for i in range(4)] + [(i + 12, i) for i in range(4)]
    return lax.ppermute(array, "ep", pairs)


def after(array, *others):
    return lax.optimization_barrier((array,) + others)[0]


def line_shards(tokens, routes, gates, w_gate, w_up, w_down):
    tok_rows, features = tokens.shape
    topk = routes.shape[1]
    experts = lax.axis_size("ep") // 2
    capacity = 2 * ((tok_rows * topk * 5 + 8 * experts - 1) // (8 * experts))
    chip = lax.axis_index("ep") // 2
    place = chip // 2
    end = (place == 0) | (place == DEPTH - 1)
    at = jnp.stack([chip, chip ^ 1, place == 0, place < DEPTH // 2, end]).astype(jnp.int32)
    block = prepare(tokens, routes, gates, experts)
    other = tuple(send(w, dc=1) for w in (w_gate, w_up, w_down))
    from_left = send(block, dz=1)
    from_right = send(block, dz=-1)

    picked, _ = compact(at, END, block, block, experts, capacity)
    first = (from_left, from_right, picked) + other
    from_left, from_right, picked, *other = lax.optimization_barrier(first)
    weights = ((w_gate, w_up, w_down), other)
    mid_left = send(from_left, dz=1)
    mid_right = send(from_right, dz=-1)
    near_picked, near = compact(at, FIRST, from_right, from_left, experts, capacity)
    near_picked = send(near_picked, dy=1)
    picked = send(picked, dy=1)
    block_out, near_out = run_expert(at, (block, near), (), weights, experts)

    far = send_far(after(block, mid_left, mid_right, block_out, near_picked))
    mid_picked, mid = compact(
        at, LOWER, mid_right, mid_left, experts, capacity, behind=(picked,)
    )
    mid_picked = send(mid_picked, dy=1)
    mid_out, back, near_back = run_expert(at, (mid,), (picked, near_picked), weights, experts)

    last_picked, last = compact(
        at, END, far, from_right, experts, capacity, behind=(near_back, mid_picked)
    )
    (mid_back,) = run_expert(at, (), (mid_picked,), weights, experts, behind=(last_picked,))
    last_picked = send(last_picked, dy=1)
    mid_back = send(after(mid_back, last_picked), dy=1)
    hidden, weight = expert_up(at, last, last_picked, weights, experts)
    mid_sum = combine(at, mid, mid_out, mid_back, 0, (), experts, behind=(hidden,))
    to_right = send(mid_sum, dz=1, only=(0, 1))
    to_left = send(mid_sum, dz=-1, only=(3, 2))
    last_out, last_back = expert_down(
        hidden, weight, last.shape[0], weights, behind=(mid_sum,)
    )
    near_back = send(after(near_back, mid_back, hidden), dy=1)
    last_back = send(after(last_back, near_back), dy=1)
    back = send(after(back, last_back, to_right, to_left), dy=1)

    near_sum = combine(at, near, near_out, near_back, 0, (), experts)
    last_sum = combine(at, last, last_out, last_back, 0, (), experts, behind=(mid_sum,))
    far_home = send_far(last_sum)
    home_left = send(merge(at, FIRST, near_sum, last_sum, to_right), dz=1)
    home_right = send(merge(at, FIRST, near_sum, near_sum, to_left), dz=-1)
    return combine(at, block, block_out, back, 0, (far_home, home_left, home_right), experts)


def partner(shard, axis, stride):
    return lax.ppermute(shard, axis, [(i, i ^ 1 << stride) for i in range(lax.axis_size(axis))])


def plain_to_grid(values):
    magnitude = jnp.abs(values)
    spacing = jnp.full(values.shape, 2.0 ** (-9), jnp.float32)
    for exponent in range(-5, 9):
        spacing = jnp.where(magnitude >= 2.0**exponent, spacing * 2.0, spacing)
    grid_value = jnp.floor(magnitude / spacing + 0.5) * spacing
    return jnp.where(values < 0, -grid_value, grid_value)


def quantize(rows):
    row_count = rows.shape[0]
    feature_count = rows.shape[1]
    blocks = rows.astype(jnp.float32).reshape(row_count, feature_count // 128, 128)
    largest = jnp.max(jnp.abs(blocks), axis=2)
    scales = ((largest + 1e-06) / 448.0).astype(jnp.bfloat16)
    scales = lax.optimization_barrier(scales)
    quantized = plain_to_grid(blocks / scales.astype(jnp.float32)[:, :, None]).astype(jnp.bfloat16)
    return (quantized.reshape(row_count, feature_count), scales)


def half_expert(quantized, scales, weights):
    row_count = quantized.shape[0]
    feature_count = quantized.shape[1]
    blocks = quantized.astype(jnp.float32).reshape(row_count, feature_count // 128, 128)
    restored = (blocks * scales.astype(jnp.float32)[:, :, None]).astype(jnp.bfloat16)
    restored = restored.reshape(row_count, feature_count)
    gate_part = jnp.dot(restored, weights[0], preferred_element_type=jnp.float32)
    up_part = jnp.dot(restored, weights[1], preferred_element_type=jnp.float32)
    hidden = (jax.nn.silu(gate_part) * up_part).astype(jnp.bfloat16)
    return jnp.dot(hidden, weights[2], preferred_element_type=jnp.float32)


def plain_expert(quantized, scales, weights):
    return half_expert(quantized, scales, weights)


def shards(tokens, routes, gates, w_gate, w_up, w_down):
    tok_rows, feature_count = tokens.shape
    topk_count = routes.shape[1]
    slices = lax.axis_size("ep")
    experts = slices // 2
    capacity = 2 * ((tok_rows * topk_count * 5 + 8 * experts - 1) // (8 * experts))
    weights = (w_gate[0], w_up[0], w_down[0])
    quantized, scales = quantize(tokens)
    qblocks = scales.shape[1]
    flat_experts = routes.reshape(-1)
    onehot = (flat_experts[:, None] == jnp.arange(experts, dtype=jnp.int32)[None, :]).astype(
        jnp.int32
    )
    rank = jnp.sum((jnp.cumsum(onehot, axis=0) - onehot) * onehot, axis=1)
    slot_index = flat_experts * capacity + rank
    token_of = jnp.arange(tok_rows * topk_count, dtype=jnp.int32) // topk_count
    table = jnp.full((experts * capacity,), tok_rows, jnp.int32).at[slot_index].set(token_of)
    padded_q = jnp.concatenate([quantized, jnp.zeros((1, feature_count), jnp.bfloat16)], axis=0)
    padded_s = jnp.concatenate([scales, jnp.zeros((1, qblocks), jnp.bfloat16)], axis=0)
    send_q = padded_q[table].reshape(experts, capacity, feature_count)
    send_s = padded_s[table].reshape(experts, capacity, qblocks)
    half_slots = capacity // 2
    split_q = send_q.reshape(slices, half_slots, feature_count)
    split_s = send_s.reshape(slices, half_slots, qblocks)
    mine_q, mine_s = (
        lax.all_to_all(split_q, "ep", split_axis=0, concat_axis=0, tiled=True),
        lax.all_to_all(split_s, "ep", split_axis=0, concat_axis=0, tiled=True),
    )
    other_q, other_s = partner((mine_q, mine_s), "ep", 0)
    leading = lax.axis_index("ep") % 2 == 0
    low_q = jnp.where(leading, mine_q, other_q)
    high_q = jnp.where(leading, other_q, mine_q)
    low_s = jnp.where(leading, mine_s, other_s)
    high_s = jnp.where(leading, other_s, mine_s)
    rows_q = jnp.concatenate([low_q, high_q], axis=1)
    rows_s = jnp.concatenate([low_s, high_s], axis=1)
    senders = rows_q.shape[0]
    partial_value = plain_expert(
        rows_q.reshape(senders * capacity, feature_count),
        rows_s.reshape(senders * capacity, qblocks),
        weights,
    )
    rounded = partial_value.astype(jnp.bfloat16).reshape(senders, capacity, feature_count)
    low_part = rounded[:, :half_slots]
    high_part = rounded[:, half_slots:]
    kept_half = jnp.where(leading, low_part, high_part)
    given_half = jnp.where(leading, high_part, low_part)
    partner_sum = partner(given_half, "ep", 0)
    kept_half = lax.optimization_barrier(kept_half)
    summed = (kept_half.astype(jnp.float32) + partner_sum.astype(jnp.float32)).astype(jnp.bfloat16)
    back = lax.all_to_all(summed, "ep", split_axis=0, concat_axis=0, tiled=True)
    expert_out = back.reshape(experts, capacity, feature_count)
    expert_out = lax.optimization_barrier(expert_out).reshape(experts * capacity, feature_count)
    picked = expert_out[slot_index].reshape(tok_rows, topk_count, feature_count)
    mixed = jnp.einsum("tk,tkd->td", gates, picked.astype(jnp.float32))
    return mixed.astype(jnp.bfloat16)


def solution(mesh):
    placed = (
        P(("groups", "ep"), None),
        P(("groups", "ep"), None),
        P(("groups", "ep"), None),
        P("ep", None, None),
        P("ep", None, None),
        P("ep", None, None),
    )
    line = mesh.shape["ep"] == 4 * DEPTH
    return jax.shard_map(
        line_shards if line else shards, mesh=mesh, in_specs=placed, out_specs=P(("groups", "ep"), None), check_vma=False
    )
```
